512 devices in a mesh: rep: 32 (over z, x), bn: 16 (over y, core).
Axes of the slice: x: 4, y: 8, z: 8, core: 2. Of those that a mesh axis runs over, the one named last changes fastest.
Arguments:
- block_input: bfloat16 [200704, 2048], P(('rep', 'bn')), may hold values from -6 to 6
- activations: bfloat16 [200704, 512], P(('rep', 'bn')), as said below
- conv_weight: bfloat16 [512, 2048], P('bn'), may hold values from -6 to 6
- bn_gain: float32 [2048], replicated, may hold values from 0.5 to 1.5
- bn_shift: float32 [2048], replicated, may hold values from -3 to 3
- out_grad: bfloat16 [200704, 2048], P(('rep', 'bn')), may hold values from -6 to 6
- velocity: float32 [512, 2048], P('bn'), may hold values from -6 to 6
Outputs:
- act_grad: bfloat16 [200704, 512], P(('rep', 'bn'))
- gain_grad: float32 [2048], replicated
- shift_grad: float32 [2048], replicated
- new_velocity: float32 [512, 2048], P('bn')
The draws below stay inside these ranges and needn't reach their ends.
Inputs may be any that keep to these rules, and one draw needn't show every extreme that they name: `activations`: entries are nonnegative.
All inputs are finite; a program needn't handle non-finite values.
Results may differ from the reference program's by a relative error of at most 0.015.
Values may be sent and summed in bfloat16 or wider, within the bound.
No kernel may reach another device: no remote copies, remote signals or barrier semaphores. Data moves between devices by JAX's collectives and lax.ppermute only.
A program may use at most 64 MiB of HBM per device.

```python
import jax
import jax.numpy as jnp
from jax import lax

CIN = 512
COUT = 2048
POS = 49
IMG_DEV = 8
BN_GROUP = 16
REPLICAS = 32
GROUP_ROWS = 6272
ROWS = 200704


def shared_draws(key):
    first = jax.random.fold_in(key, 0)
    third = jax.random.fold_in(key, 2)
    normal_part = jax.random.normal(first, (ROWS, CIN), jnp.float32)
    underlying = normal_part
    block_width = CIN // BN_GROUP
    block_start = jax.random.randint(third, (), 0, BN_GROUP) * block_width
    stride = max(block_width // 8, 1)
    chosen = block_start + jnp.arange(8) * stride % block_width
    return (underlying, chosen.astype(jnp.int32))


def draw_activations(key, part):
    underlying, chosen = shared_draws(key)
    key = jax.random.fold_in(key, 11)
    second, third = jax.random.split(key, 2)
    images = ROWS // POS
    image_index = jnp.arange(images) // IMG_DEV
    place = (image_index % BN_GROUP).astype(jnp.float32)
    slope = 1.0 + 2.0 * place / (BN_GROUP - 1)
    jitter = jnp.exp(jax.random.uniform(second, (images,), jnp.float32, -0.35, 0.35))
    row_scale = jnp.repeat(slope * jitter, POS)
    channel = jnp.exp(jax.random.uniform(third, (CIN,), jnp.float32, 0.0, 2.3))
    values = jnp.maximum(underlying, 0.0) * row_scale[:, None] * channel[None, :]
    return values.astype(jnp.bfloat16)


def draw_out_grad(key, part):
    underlying, chosen = shared_draws(key)
    key = jax.random.fold_in(key, 23)
    noise_key, vector_key = jax.random.split(key, 2)
    noise = jax.random.normal(noise_key, (ROWS, COUT), jnp.float32)
    vectors = jnp.clip(jax.random.normal(vector_key, (8, COUT), jnp.float32), -3.0, 3.0)
    picked = jnp.take(underlying, chosen, axis=1)
    coherent = jnp.zeros((ROWS, COUT), jnp.float32)
    for term in range(8):
        coherent = coherent + picked[:, term:term + 1] * vectors[term][None, :]
    values = jnp.clip(noise + 0.025 * coherent, -6.0, 6.0)
    return values.astype(jnp.bfloat16)


def steps_of(key, shape, shards, smallest, top_value):
    def one(axis_at, shards_of):
        steps = jax.random.uniform(jax.random.fold_in(jax.random.fold_in(key, 6), axis_at), (shards_of,), jnp.float32, smallest / len(shards), top_value / len(shards))
        return jnp.repeat(jnp.exp(steps), shape[axis_at] // shards_of).reshape((-1,) + (1,) * (len(shape) - axis_at - 1))

    level = one(*shards[0])
    for cut in shards[1:]:
        level = level * one(*cut)
    return level


def gaussian(stream_key, dims, spread, bound, cuts=(), kind=jnp.bfloat16):
    array = spread * jax.random.normal(stream_key, dims, jnp.float32)
    if cuts:
        array = array * steps_of(stream_key, dims, cuts, -0.22, 0.18)
    return jnp.clip(array, -bound, bound).astype(kind)


def setup_inputs(seed: int = 0) -> dict:
    key_list = jax.random.split(jax.random.key(seed), 8)
    block_input = gaussian(key_list[0], (ROWS, COUT), 1.0, 6.0, ((0, 512),))
    activations = draw_activations(jax.random.fold_in(key_list[7], 71), 0)
    conv_weight = gaussian(key_list[2], (CIN, COUT), 1.0, 6.0, ((0, 16),))
    bn_gain = jnp.clip(1.0 + 0.1 * jax.random.normal(key_list[3], (COUT,), jnp.float32), 0.5, 1.5)
    bn_shift = gaussian(key_list[4], (COUT,), 0.5, 3.0, (), jnp.float32)
    out_grad = draw_out_grad(jax.random.fold_in(key_list[7], 71), 0)
    velocity = gaussian(key_list[6], (CIN, COUT), 1.0, 6.0, ((0, 16),), jnp.float32)
    return {"block_input": block_input, "activations": activations, "conv_weight": conv_weight, "bn_gain": bn_gain, "bn_shift": bn_shift, "out_grad": out_grad, "velocity": velocity}


epsilon = 1e-05
weight_decay = 5e-05
momentum = 0.9

def reference(block_input, activations, conv_weight, bn_gain, bn_shift, out_grad, velocity):
    groups_in = block_input.reshape(REPLICAS, GROUP_ROWS, COUT)
    groups_act = activations.reshape(REPLICAS, GROUP_ROWS, CIN)
    groups_grad = out_grad.reshape(REPLICAS, GROUP_ROWS, COUT)

    def group_pass(carry, item):
        weight_acc, gain_acc, shift_acc = carry
        residual, acts, incoming = item
        conv_out = jnp.dot(acts, conv_weight, preferred_element_type=jnp.float32)
        chan_mean = lax.optimization_barrier(jnp.sum(conv_out, axis=0)) / GROUP_ROWS
        centered = conv_out - chan_mean
        variance = lax.optimization_barrier(jnp.sum(centered * centered, axis=0)) / GROUP_ROWS
        inv_std = lax.rsqrt(variance + epsilon)
        normed = centered * inv_std
        summed = bn_gain * normed + bn_shift + residual.astype(jnp.float32)
        grad_pre = jnp.where(summed > 0.0, incoming.astype(jnp.float32), jnp.zeros_like(summed))
        sum_grad = lax.optimization_barrier(jnp.sum(grad_pre, axis=0))
        sum_cross = lax.optimization_barrier(jnp.sum(grad_pre * normed, axis=0))
        grad_conv = (bn_gain * inv_std * (grad_pre - sum_grad / GROUP_ROWS - normed * (sum_cross / GROUP_ROWS))).astype(jnp.bfloat16)
        grad_acts = lax.dot_general(grad_conv, conv_weight, (((1,), (1,)), ((), ())), preferred_element_type=jnp.float32).astype(jnp.bfloat16)
        weight_acc = weight_acc + lax.dot_general(acts, grad_conv, (((0,), (0,)), ((), ())), preferred_element_type=jnp.float32)
        return ((weight_acc, gain_acc + sum_cross, shift_acc + sum_grad), grad_acts)
    start = (jnp.zeros((CIN, COUT), jnp.float32), jnp.zeros((COUT,), jnp.float32), jnp.zeros((COUT,), jnp.float32))
    totals, grad_blocks = lax.scan(group_pass, start, (groups_in, groups_act, groups_grad))
    weight_grad, gain_grad, shift_grad = totals
    act_grad = grad_blocks.reshape(ROWS, CIN)
    weight_f = conv_weight.astype(jnp.float32)
    weight_norm = jnp.sqrt(jnp.sum(weight_f * weight_f))
    grad_norm = jnp.sqrt(jnp.sum(weight_grad * weight_grad))
    ratio = weight_norm / (grad_norm + weight_decay * weight_norm)
    new_velocity = momentum * velocity + ratio * (weight_grad + weight_decay * weight_f)
    return (act_grad, gain_grad, shift_grad, new_velocity)
```

```python
import jax
import jax.numpy as jnp
from jax import lax
from jax.sharding import Mesh, PartitionSpec as P

epsilon = 1e-05
weight_decay = 5e-05
momentum = 0.9
f32, bf16 = jnp.float32, jnp.bfloat16
rep = ("z", "x")
bn = ("y", "c")


def swap(value):
    return lax.ppermute(value, "c", [(0, 1), (1, 0)])


def exchange(pieces, axis):
    return lax.all_to_all(pieces, axis, 0, 0, tiled=True)


def copies(value, axis):
    n = lax.axis_size(axis)
    return exchange(jnp.broadcast_to(value[None], (n, *value.shape)), axis)


def split(value):
    high = value.astype(bf16)
    return high, (value - high.astype(f32)).astype(bf16)


def local(block_input, activations, conv_weight, bn_gain, bn_shift, out_grad, velocity):
    rows, cin = activations.shape
    part, cout = conv_weight.shape
    nz, nx, ny = lax.axis_size("z"), lax.axis_size("x"), lax.axis_size("y")
    core = lax.axis_index("c")
    group_rows = rows * lax.axis_size(bn)
    lanes = 128

    own = copies(conv_weight, "y")
    other = swap(own)
    first = jnp.where(core == 0, own, other)
    second = jnp.where(core == 0, other, own)
    full_weight = jnp.stack([first, second], axis=1).reshape(cin, cout)

    conv_out = jnp.dot(activations, full_weight, preferred_element_type=f32)
    local_mean = jnp.sum(conv_out, axis=0) / rows
    spread = conv_out - local_mean
    local_square = jnp.sum(spread * spread, axis=0)
    moments = jnp.stack([local_mean, local_square]).reshape(-1, lanes)
    moments = copies(moments, bn).reshape(-1, 2, cout)
    chan_mean = jnp.mean(moments[:, 0], axis=0)
    offset = moments[:, 0] - chan_mean
    variance = (jnp.sum(moments[:, 1], axis=0) + rows * jnp.sum(offset * offset, axis=0)) / group_rows
    inv_std = lax.rsqrt(variance + epsilon)

    normed = (conv_out - chan_mean) * inv_std
    summed = bn_gain * normed + bn_shift + block_input.astype(f32)
    grad_pre = jnp.where(summed > 0.0, out_grad.astype(f32), jnp.zeros_like(summed))
    stats = jnp.stack([jnp.sum(grad_pre, axis=0), jnp.sum(grad_pre * normed, axis=0)])
    stats = jnp.sum(copies(stats.reshape(-1, lanes), bn), axis=0).reshape(2, cout)
    sum_grad, sum_cross = stats[0], stats[1]
    grad_conv = (
        bn_gain * inv_std * (grad_pre - sum_grad / group_rows - normed * (sum_cross / group_rows))
    ).astype(bf16)

    partial = lax.dot_general(
        activations, grad_conv, (((0,), (0,)), ((), ())), preferred_element_type=f32
    ).astype(bf16)
    partial = partial.reshape(ny, 2, part, cout)
    mine = jnp.where(core == 0, partial[:, 0], partial[:, 1])
    theirs = jnp.where(core == 0, partial[:, 1], partial[:, 0])
    pair = (mine.astype(f32) + swap(theirs).astype(f32)).astype(bf16)
    pair = pair.reshape(ny, nx, part // nx, nz, cout // nz).transpose(3, 1, 0, 2, 4)
    pair = pair.reshape(nz * nx, cin // 2 // nx, cout // nz)
    grad_high, grad_low = split(sum_grad)
    cross_high, cross_low = split(sum_cross)
    tail = jnp.stack([grad_high, grad_low, cross_high, cross_low])
    tail = tail.reshape(nx, nz, 1, cout // nz).transpose(1, 0, 2, 3).reshape(nz * nx, 1, cout // nz)
    tail = jnp.pad(tail, ((0, 0), (0, 7), (0, 0)))
    summed_rep = jnp.sum(exchange(jnp.concatenate([pair, tail], axis=1), rep).astype(f32), axis=0)
    act_grad = lax.dot_general(
        grad_conv, full_weight, (((1,), (1,)), ((), ())), preferred_element_type=f32
    ).astype(bf16)
    block = summed_rep[: cin // 2 // nx].reshape(ny, part // nx, cout // nz)
    piece = jnp.sum(exchange(block, "y"), axis=0)
    tail_high, tail_low = split(summed_rep[cin // 2 // nx])
    low_rows = jnp.pad(jnp.stack([tail_high, tail_low]), ((0, 6), (0, 0)))
    whole = copies(jnp.concatenate([piece.astype(bf16), low_rows]), rep).astype(f32)
    whole = whole.reshape(nz, nx, -1, cout // nz)
    weight_grad = whole[:, :, : part // nx].transpose(1, 2, 0, 3).reshape(part, cout)
    totals = jnp.sum(whole[:, :, part // nx : part // nx + 2], axis=2)
    totals = totals.transpose(1, 0, 2).reshape(nx, cout)
    shift_grad = totals[0] + totals[1]
    gain_grad = totals[2] + totals[3]

    weight_f = conv_weight.astype(f32)
    full_f = full_weight.astype(f32)
    weight_norm = jnp.sqrt(jnp.sum(full_f * full_f))
    square = jnp.sum(weight_grad * weight_grad)
    squares = copies(jnp.broadcast_to(square, (8, lanes)), bn).reshape(-1, 8, lanes)
    grad_norm = jnp.sqrt(jnp.sum(squares[:, 0, 0]))
    ratio = weight_norm / (grad_norm + weight_decay * weight_norm)
    new_velocity = momentum * velocity + ratio * (weight_grad + weight_decay * weight_f)
    return (act_grad, gain_grad, shift_grad, new_velocity)


def solution(mesh, shape=(8, 4, 8, 2)):
    fine = Mesh(mesh.devices.reshape(shape), ("z", "x", "y", "c"))
    every = P(("z", "x", "y", "c"), None)
    return jax.shard_map(
        local,
        mesh=fine,
        in_specs=(every, every, P(bn, None), P(), P(), every, P(bn, None)),
        out_specs=(every, P(), P(), P(bn, None)),
        check_vma=False,
    )
```

```python
import jax
import jax.numpy as jnp
from jax import lax
from jax.experimental import pallas as pl
from jax.experimental.pallas import tpu as pltpu
from jax.sharding import Mesh, PartitionSpec as P

epsilon = 1e-05
weight_decay = 5e-05
momentum = 0.9
f32, bf16 = jnp.float32, jnp.bfloat16
rep = ("z", "x")
bn = ("y", "c")
lanes = 128
chunk = 512
groups = chunk // lanes


def swap(value):
    return lax.ppermute(value, "c", [(0, 1), (1, 0)])


def exchange(pieces, axis):
    return lax.all_to_all(pieces, axis, 0, 0, tiled=True)


def copies(value, axis):
    n = lax.axis_size(axis)
    return exchange(jnp.broadcast_to(value[None], (n, *value.shape)), axis)


def fold(row):
    return [row[:, q * lanes : (q + 1) * lanes] for q in range(groups)]


def unfold(tile):
    return jnp.concatenate([tile[q : q + 1] for q in range(groups)], axis=1)


def high_low(value):
    high = value.astype(bf16).astype(f32)
    return high, value - high


def moments_kernel(acts, own, other, weight, conv, moments):
    core = lax.axis_index("c")
    count, part, _ = own.shape
    for y in range(count):
        at = pl.multiple_of((2 * y + core) * part, part)
        weight[pl.ds(at, part), :] = own[y]
        at = pl.multiple_of((2 * y + 1 - core) * part, part)
        weight[pl.ds(at, part), :] = other[y]
    out = jnp.dot(acts[...], weight[...], preferred_element_type=f32)
    conv[...] = out
    mean = jnp.sum(out, axis=0, keepdims=True) / out.shape[0]
    spread = out - mean
    square = jnp.sum(spread * spread, axis=0, keepdims=True)
    tile = jnp.concatenate(fold(mean) + fold(square), axis=0)
    moments[...] = jnp.broadcast_to(tile[None], moments.shape)


def pooled(moments, rows):
    members = moments.shape[0]
    means, squares = moments[:, :groups], moments[:, groups:]
    mean = jnp.sum(means, axis=0) / members
    offset = means - mean[None]
    square = jnp.sum(squares, axis=0) + rows * jnp.sum(offset * offset, axis=0)
    inv_std = lax.rsqrt(square / (rows * members) + epsilon)
    return unfold(mean), unfold(inv_std)


def stats_kernel(conv, moments, gain, shift, block_input, out_grad, grad, stats):
    mean, inv_std = pooled(moments[...], conv.shape[0])
    centered = conv[...] - mean
    summed = centered * (gain[...] * inv_std) + shift[...] + block_input[...].astype(f32)
    value = jnp.where(summed > 0.0, out_grad[...].astype(f32), 0.0)
    grad[...] = value.astype(bf16)
    sum_grad = jnp.sum(value, axis=0, keepdims=True)
    sum_cross = jnp.sum(value * centered, axis=0, keepdims=True) * inv_std
    tile = jnp.concatenate(fold(sum_grad) + fold(sum_cross), axis=0)
    stats[...] = jnp.broadcast_to(tile[None], stats.shape)


def weight_kernel(conv, moments, stats, gain, grad, acts_t, grad_conv, mine, theirs, tail, wide):
    core = lax.axis_index("c")
    rows = conv.shape[0]
    group_rows = rows * moments.shape[0]
    mean, inv_std = pooled(moments[...], rows)
    sums = jnp.sum(stats[...], axis=0)
    sum_grad, sum_cross = sums[:groups], sums[groups:]
    shift = unfold(sum_grad) / group_rows
    slope = inv_std * unfold(sum_cross) / group_rows
    value = grad[...].astype(f32) - shift - (conv[...] - mean) * slope
    narrow = (gain[...] * inv_std * value).astype(bf16)
    grad_conv[...] = narrow
    wide[...] = jnp.dot(acts_t[...], narrow, preferred_element_type=f32)
    nz, nx, length, _ = mine.shape
    part = 8 * nx
    ny = wide.shape[0] // (2 * part)
    halves = chunk // nz // lanes
    for z in range(nz):
        for x in range(nx):
            for out, owner in ((mine, core), (theirs, 1 - core)):
                rows_of = [
                    wide[
                        pl.ds(pl.multiple_of((2 * y + owner) * part + 8 * x, 8), 8),
                        pl.ds((z * halves + h) * lanes, lanes),
                    ]
                    for h in range(halves)
                    for y in range(ny)
                ]
                out[z, x] = jnp.concatenate(rows_of, axis=0).astype(bf16)
    planes = (*high_low(sum_grad), *high_low(sum_cross))
    for z in range(nz):
        for x in range(nx):
            rows_of = planes[x][z * halves : (z + 1) * halves]
            tail[z, x] = jnp.concatenate([rows_of, jnp.zeros((8 - halves, lanes), f32)], axis=0)


def act_kernel(grad_conv, weight, act_grad, squares, total):
    step = pl.program_id(0)
    term = lax.dot_general(
        grad_conv[...], weight[...], (((1,), (1,)), ((), ())), preferred_element_type=f32
    )
    wide = weight[...].astype(f32)
    square = jnp.sum((wide * wide).reshape(-1, 8, wide.shape[1]), axis=0)
    square = sum(fold(square))

    @pl.when(step == 0)
    def _():
        total[...] = term
        squares[...] = square

    @pl.when(step > 0)
    def _():
        total[...] += term
        squares[...] += square

    act_grad[...] = total[...].astype(bf16)


def total_kernel(partial, tail, out, total):
    ny = partial.shape[0]
    halves = tail.shape[0]
    total[...] = jnp.sum(partial[...].astype(f32), axis=0)
    value = total[...]
    square = jnp.sum(jnp.sum(value * value, axis=0, keepdims=True), axis=1, keepdims=True)
    square = jnp.broadcast_to(square, (1, lanes))
    y = lax.axis_index("y")
    own = [total[pl.ds(pl.multiple_of((h * ny + y) * 8, 8), 8), :] for h in range(halves)]
    extra = [*high_low(tail[...]), *high_low(square)]
    used = sum(e.shape[0] for e in extra)
    extra.append(jnp.zeros((8 - used, lanes), f32))
    tile = jnp.concatenate(own + extra, axis=0).astype(bf16)
    out[...] = jnp.broadcast_to(tile[None], out.shape)


def shape(dims, dtype):
    return jax.ShapeDtypeStruct(dims, dtype)


def whole(dims):
    return pl.BlockSpec(dims, lambda j: (0,) * len(dims))


def across(dims, axis):
    return pl.BlockSpec(dims, lambda j: tuple(j if a == axis else 0 for a in range(len(dims))))


def params(mib=24):
    return pltpu.CompilerParams(vmem_limit_bytes=mib << 20)


def local(block_input, activations, conv_weight, bn_gain, bn_shift, out_grad, velocity):
    rows, cin = activations.shape
    part, cout = conv_weight.shape
    nz, nx, ny = lax.axis_size("z"), lax.axis_size("x"), lax.axis_size("y")
    members = lax.axis_size(bn)
    steps = cout // chunk
    gain, shift = bn_gain.reshape(1, cout), bn_shift.reshape(1, cout)
    acts_t = activations.T
    per = nz // steps
    halves = cout // nz // lanes
    length = halves * ny * 8

    own = copies(conv_weight, "y").reshape(ny, part, cout)
    other = swap(own)
    tile = shape((members, steps * 8, lanes), f32)
    wide_block = across((rows, chunk), 1)
    tile_block = across((members, 8, lanes), 1)
    row_block = across((1, chunk), 1)
    weight, conv, moments = pl.pallas_call(
        moments_kernel,
        grid=(steps,),
        in_specs=[whole((rows, cin)), across((ny, part, chunk), 2), across((ny, part, chunk), 2)],
        out_specs=[across((cin, chunk), 1), wide_block, tile_block],
        out_shape=[shape((cin, cout), bf16), shape((rows, cout), f32), tile],
        compiler_params=params(),
        name="moments",
    )(activations, own, other)
    moments = exchange(moments, bn)

    grad, stats = pl.pallas_call(
        stats_kernel,
        grid=(steps,),
        in_specs=[wide_block, tile_block, row_block, row_block, wide_block, wide_block],
        out_specs=[wide_block, tile_block],
        out_shape=[shape((rows, cout), bf16), tile],
        compiler_params=params(),
        name="stats",
    )(conv, moments, gain, shift, block_input, out_grad)
    stats = exchange(stats, bn)

    piece = shape((nz, nx, length, lanes), bf16)
    piece_block = across((per, nx, length, lanes), 0)
    grad_conv, mine, theirs, tail = pl.pallas_call(
        weight_kernel,
        grid=(steps,),
        in_specs=[wide_block, tile_block, tile_block, row_block, wide_block, whole((cin, rows))],
        out_specs=[wide_block, piece_block, piece_block, across((per, nx, 8, lanes), 0)],
        out_shape=[shape((rows, cout), bf16), piece, piece, shape((nz, nx, 8, lanes), f32)],
        scratch_shapes=[pltpu.VMEM((cin, chunk), f32)],
        compiler_params=params(),
        name="weight_partial",
    )(conv, moments, stats, gain, grad, acts_t)
    pair = (mine.astype(f32) + swap(theirs).astype(f32)).astype(bf16)
    pair = jnp.concatenate([pair, tail.astype(bf16)], axis=2).reshape(nz * nx, length + 8, lanes)
    received = exchange(pair, rep)
    act_grad, squares = pl.pallas_call(
        act_kernel,
        grid=(steps,),
        in_specs=[wide_block, across((cin, chunk), 1)],
        out_specs=[whole((rows, cin)), whole((8, lanes))],
        out_shape=[shape((rows, cin), bf16), shape((8, lanes), f32)],
        scratch_shapes=[pltpu.VMEM((rows, cin), f32)],
        compiler_params=params(),
        cost_estimate=pl.CostEstimate(
            flops=2 * rows * cin * cout, bytes_accessed=2 * (rows + cin) * cout, transcendentals=0
        ),
        name="act_grad",
    )(grad_conv, weight)
    summed = jnp.sum(received.astype(f32), axis=0)
    blocks = copies(summed[:length].astype(bf16), "y")
    blocks = blocks.reshape(ny, length, lanes)
    depth = halves * 8 + 8
    ready = pl.pallas_call(
        total_kernel,
        grid=(1,),
        in_specs=[whole((ny, length, lanes)), whole((halves, lanes))],
        out_specs=whole((nz * nx, depth, lanes)),
        out_shape=shape((nz * nx, depth, lanes), bf16),
        scratch_shapes=[pltpu.VMEM((length, lanes), f32)],
        compiler_params=params(),
        name="totals",
    )(blocks, summed[length : length + halves])
    everything = exchange(ready, rep).astype(f32)

    at = halves * 8
    square = jnp.sum(everything[:, at + 2 * halves : at + 2 * halves + 2, 0])
    square_other = swap(jnp.broadcast_to(square, (8, lanes)))[0, 0]
    grid = everything.reshape(nz, nx, depth, lanes)
    weight_grad = grid[:, :, :at].reshape(nz, nx, halves, 8, lanes)
    weight_grad = weight_grad.transpose(1, 3, 0, 2, 4).reshape(part, cout)
    totals = grid[:, :, at : at + halves] + grid[:, :, at + halves : at + 2 * halves]
    totals = totals.transpose(1, 0, 2, 3).reshape(nx, cout)
    shift_grad = totals[0] + totals[1]
    gain_grad = totals[2] + totals[3]

    weight_f = conv_weight.astype(f32)
    weight_norm = jnp.sqrt(jnp.sum(squares))
    grad_norm = jnp.sqrt(square + square_other)
    ratio = weight_norm / (grad_norm + weight_decay * weight_norm)
    new_velocity = momentum * velocity + ratio * (weight_grad + weight_decay * weight_f)
    return (act_grad, gain_grad, shift_grad, new_velocity)


def solution(mesh, dims=(8, 4, 8, 2)):
    fine = Mesh(mesh.devices.reshape(dims), ("z", "x", "y", "c"))
    every = P(("z", "x", "y", "c"), None)
    return jax.shard_map(
        local,
        mesh=fine,
        in_specs=(every, every, P(bn, None), P(), P(), every, P(bn, None)),
        out_specs=(every, P(), P(), P(bn, None)),
        check_vma=False,
    )
```

```python
import functools

import jax
import jax.numpy as jnp
from jax import lax
from jax.experimental import pallas as pl
from jax.experimental.pallas import tpu as pltpu
from jax.sharding import Mesh, PartitionSpec as P

epsilon = 1e-05
weight_decay = 5e-05
momentum = 0.9
f32, bf16 = jnp.float32, jnp.bfloat16
rep = ("z", "x")
bn = ("y", "c")
lanes = 128
chunk = 512
groups = chunk // lanes


def swap(value):
    return lax.ppermute(value, "c", [(0, 1), (1, 0)])


def exchange(pieces, axis):
    return lax.all_to_all(pieces, axis, 0, 0, tiled=True)


def copies(value, axis):
    n = lax.axis_size(axis)
    return exchange(jnp.broadcast_to(value[None], (n, *value.shape)), axis)


def fold(row):
    return [row[:, q * lanes : (q + 1) * lanes] for q in range(groups)]


def unfold(tile):
    return jnp.concatenate([tile[q : q + 1] for q in range(groups)], axis=1)


def high_low(value):
    high = value.astype(bf16).astype(f32)
    return high, value - high


def moments_kernel(acts, own, other, weight, conv, moments):
    core = lax.axis_index("c")
    count, part, _ = own.shape
    for y in range(count):
        at = pl.multiple_of((2 * y + core) * part, part)
        weight[pl.ds(at, part), :] = own[y]
        at = pl.multiple_of((2 * y + 1 - core) * part, part)
        weight[pl.ds(at, part), :] = other[y]
    out = jnp.dot(acts[...], weight[...], preferred_element_type=f32)
    conv[...] = out
    mean = jnp.sum(out, axis=0, keepdims=True) / out.shape[0]
    spread = out - mean
    square = jnp.sum(spread * spread, axis=0, keepdims=True)
    tile = jnp.concatenate(fold(mean) + fold(square), axis=0)
    moments[...] = jnp.broadcast_to(tile[None], moments.shape)


def pooled(moments, rows):
    members = moments.shape[0]
    means, squares = moments[:, :groups], moments[:, groups:]
    mean = jnp.sum(means, axis=0) / members
    offset = means - mean[None]
    square = jnp.sum(squares, axis=0) + rows * jnp.sum(offset * offset, axis=0)
    inv_std = lax.rsqrt(square / (rows * members) + epsilon)
    return unfold(mean), unfold(inv_std)


def stats_kernel(conv, moments, gain, shift, block_input, out_grad, grad, stats):
    mean, inv_std = pooled(moments[...], conv.shape[0])
    centered = conv[...] - mean
    summed = centered * (gain[...] * inv_std) + shift[...] + block_input[...].astype(f32)
    value = jnp.where(summed > 0.0, out_grad[...].astype(f32), 0.0)
    grad[...] = value.astype(bf16)
    sum_grad = jnp.sum(value, axis=0, keepdims=True)
    sum_cross = jnp.sum(value * centered, axis=0, keepdims=True) * inv_std
    tile = jnp.concatenate(fold(sum_grad) + fold(sum_cross), axis=0)
    stats[...] = jnp.broadcast_to(tile[None], stats.shape)


def weight_kernel(
    conv, moments, stats, gain, grad, acts, grad_conv, mine, theirs, tail, wide, acts_t
):
    core = lax.axis_index("c")
    rows = conv.shape[0]
    group_rows = rows * moments.shape[0]
    mean, inv_std = pooled(moments[...], rows)
    sums = jnp.sum(stats[...], axis=0)
    sum_grad, sum_cross = sums[:groups], sums[groups:]
    shift = unfold(sum_grad) / group_rows
    slope = inv_std * unfold(sum_cross) / group_rows
    value = grad[...].astype(f32) - shift - (conv[...] - mean) * slope
    narrow = (gain[...] * inv_std * value).astype(bf16)
    grad_conv[...] = narrow

    @pl.when(pl.program_id(0) == 0)
    def _():
        acts_t[...] = acts[...].T

    wide[...] = jnp.dot(acts_t[...], narrow, preferred_element_type=f32)
    nz, nx, length, _ = mine.shape
    part = 8 * nx
    ny = wide.shape[0] // (2 * part)
    halves = chunk // nz // lanes
    for z in range(nz):
        for x in range(nx):
            for out, owner in ((mine, core), (theirs, 1 - core)):
                rows_of = [
                    wide[
                        pl.ds(pl.multiple_of((2 * y + owner) * part + 8 * x, 8), 8),
                        pl.ds((z * halves + h) * lanes, lanes),
                    ]
                    for h in range(halves)
                    for y in range(ny)
                ]
                out[z, x] = jnp.concatenate(rows_of, axis=0).astype(bf16)
    planes = (*high_low(sum_grad), *high_low(sum_cross))
    for z in range(nz):
        for x in range(nx):
            rows_of = planes[x][z * halves : (z + 1) * halves]
            tail[z, x] = jnp.concatenate([rows_of, jnp.zeros((8 - halves, lanes), f32)], axis=0)


def act_kernel(grad_conv, weight, act_grad, squares, total):
    step = pl.program_id(0)
    term = lax.dot_general(
        grad_conv[...], weight[...], (((1,), (1,)), ((), ())), preferred_element_type=f32
    )
    wide = weight[...].astype(f32)
    square = jnp.sum((wide * wide).reshape(-1, 8, wide.shape[1]), axis=0)
    square = sum(fold(square))

    @pl.when(step == 0)
    def _():
        total[...] = term
        squares[...] = square

    @pl.when(step > 0)
    def _():
        total[...] += term
        squares[...] += square

    act_grad[...] = total[...].astype(bf16)


def total_kernel(partial, summed, out, total):
    ny, length, _ = partial.shape
    halves = length // (8 * ny)
    total[...] = jnp.sum(partial[...].astype(f32), axis=0)
    value = total[...]
    square = jnp.sum(jnp.sum(value * value, axis=0, keepdims=True), axis=1, keepdims=True)
    square = jnp.broadcast_to(square, (1, lanes))
    y = lax.axis_index("y")
    own = [total[pl.ds(pl.multiple_of((h * ny + y) * 8, 8), 8), :] for h in range(halves)]
    extra = [*high_low(summed[length : length + halves, :]), *high_low(square)]
    used = sum(e.shape[0] for e in extra)
    extra.append(jnp.zeros((8 - used, lanes), f32))
    tile = jnp.concatenate(own + extra, axis=0).astype(bf16)
    out[...] = jnp.broadcast_to(tile[None], out.shape)


def step_kernel(nx, parts, squares, weight_squares, weight, velocity, out, gain, shift):
    nz = parts.shape[0] // nx
    halves = out.shape[1] // nz // lanes
    grad_square = jnp.sum(squares[...], axis=0, keepdims=True)[:, :1]
    weight_square = jnp.sum(weight_squares[...], axis=0, keepdims=True)
    weight_square = jnp.sum(weight_square, axis=1, keepdims=True)
    weight_norm = jnp.sqrt(weight_square)
    ratio = weight_norm / (jnp.sqrt(grad_square) + weight_decay * weight_norm)
    at = 8 * halves
    for z in range(nz):
        values = [parts[z * nx + x].astype(f32) for x in range(nx)]
        for h in range(halves):
            cols = pl.ds((z * halves + h) * lanes, lanes)
            weight_grad = jnp.concatenate([v[8 * h : 8 * h + 8] for v in values], axis=0)
            decayed = weight_grad + weight_decay * weight[:, cols].astype(f32)
            out[:, cols] = momentum * velocity[:, cols] + ratio * decayed
            sums = [v[at + h : at + h + 1] + v[at + halves + h : at + halves + h + 1] for v in values]
            shift[:, cols] = sums[0] + sums[1]
            gain[:, cols] = sums[2] + sums[3]


def shape(dims, dtype):
    return jax.ShapeDtypeStruct(dims, dtype)


def whole(dims):
    return pl.BlockSpec(dims, lambda j: (0,) * len(dims))


def across(dims, axis):
    return pl.BlockSpec(dims, lambda j: tuple(j if a == axis else 0 for a in range(len(dims))))


def params(mib=24):
    return pltpu.CompilerParams(vmem_limit_bytes=mib << 20)


def local(block_input, activations, conv_weight, bn_gain, bn_shift, out_grad, velocity):
    rows, cin = activations.shape
    part, cout = conv_weight.shape
    nz, nx, ny = lax.axis_size("z"), lax.axis_size("x"), lax.axis_size("y")
    members = lax.axis_size(bn)
    steps = cout // chunk
    gain, shift = bn_gain.reshape(1, cout), bn_shift.reshape(1, cout)
    per = nz // steps
    halves = cout // nz // lanes
    length = halves * ny * 8

    own = copies(conv_weight, "y").reshape(ny, part, cout)
    other = swap(own)
    tile = shape((members, steps * 8, lanes), f32)
    wide_block = across((rows, chunk), 1)
    tile_block = across((members, 8, lanes), 1)
    row_block = across((1, chunk), 1)
    weight, conv, moments = pl.pallas_call(
        moments_kernel,
        grid=(steps,),
        in_specs=[whole((rows, cin)), across((ny, part, chunk), 2), across((ny, part, chunk), 2)],
        out_specs=[across((cin, chunk), 1), wide_block, tile_block],
        out_shape=[pltpu.HBM((cin, cout), bf16), shape((rows, cout), f32), tile],
        compiler_params=params(),
        name="moments",
    )(activations, own, other)
    moments = exchange(moments, bn)

    grad, stats = pl.pallas_call(
        stats_kernel,
        grid=(steps,),
        in_specs=[wide_block, tile_block, row_block, row_block, wide_block, wide_block],
        out_specs=[wide_block, tile_block],
        out_shape=[shape((rows, cout), bf16), tile],
        compiler_params=params(),
        name="stats",
    )(conv, moments, gain, shift, block_input, out_grad)
    stats = exchange(stats, bn)

    piece = shape((nz, nx, length, lanes), bf16)
    piece_block = across((per, nx, length, lanes), 0)
    grad_conv, mine, theirs, tail = pl.pallas_call(
        weight_kernel,
        grid=(steps,),
        in_specs=[wide_block, tile_block, tile_block, row_block, wide_block, whole((rows, cin))],
        out_specs=[wide_block, piece_block, piece_block, across((per, nx, 8, lanes), 0)],
        out_shape=[pltpu.HBM((rows, cout), bf16), piece, piece, shape((nz, nx, 8, lanes), f32)],
        scratch_shapes=[pltpu.VMEM((cin, chunk), f32), pltpu.VMEM((cin, rows), bf16)],
        compiler_params=params(),
        name="weight_partial",
    )(conv, moments, stats, gain, grad, activations)
    pair = (mine.astype(f32) + swap(theirs).astype(f32)).astype(bf16)
    pair = jnp.concatenate([pair, tail.astype(bf16)], axis=2).reshape(nz * nx, length + 8, lanes)
    received = exchange(pair, rep)
    act_grad, squares = pl.pallas_call(
        act_kernel,
        grid=(steps,),
        in_specs=[wide_block, across((cin, chunk), 1)],
        out_specs=[whole((rows, cin)), whole((8, lanes))],
        out_shape=[shape((rows, cin), bf16), shape((8, lanes), f32)],
        scratch_shapes=[pltpu.VMEM((rows, cin), f32)],
        compiler_params=params(),
        cost_estimate=pl.CostEstimate(
            flops=2 * rows * cin * cout, bytes_accessed=2 * (rows + cin) * cout, transcendentals=0
        ),
        name="act_grad",
    )(grad_conv, weight)
    summed = jnp.sum(received.astype(f32), axis=0)
    blocks = copies(summed[:length].astype(bf16), "y")
    blocks = blocks.reshape(ny, length, lanes)
    depth = halves * 8 + 8
    ready = pl.pallas_call(
        total_kernel,
        grid=(1,),
        in_specs=[whole((ny, length, lanes)), whole((length + 8, lanes))],
        out_specs=whole((nz * nx, depth, lanes)),
        out_shape=shape((nz * nx, depth, lanes), bf16),
        scratch_shapes=[pltpu.VMEM((length, lanes), f32)],
        compiler_params=params(),
        name="totals",
    )(blocks, summed)
    ready = exchange(ready, rep)
    at = halves * 8 + 2 * halves
    square = jnp.sum(ready[:, at : at + 2].astype(f32), axis=(0, 1))
    square = lax.all_gather(square, "c")
    new_velocity, gain_grad, shift_grad = pl.pallas_call(
        functools.partial(step_kernel, nx),
        grid=(1,),
        in_specs=[
            whole((nz * nx, depth, lanes)),
            whole((2, lanes)),
            whole((8, lanes)),
            whole((part, cout)),
            whole((part, cout)),
        ],
        out_specs=[whole((part, cout)), whole((1, cout)), whole((1, cout))],
        out_shape=[shape((part, cout), f32), shape((1, cout), f32), shape((1, cout), f32)],
        compiler_params=params(),
        name="step",
    )(ready, square, squares, conv_weight, velocity)
    return (act_grad, gain_grad.reshape(cout), shift_grad.reshape(cout), new_velocity)


def solution(mesh, dims=(8, 4, 8, 2)):
    fine = Mesh(mesh.devices.reshape(dims), ("z", "x", "y", "c"))
    every = P(("z", "x", "y", "c"), None)
    return jax.shard_map(
        local,
        mesh=fine,
        in_specs=(every, every, P(bn, None), P(), P(), every, P(bn, None)),
        out_specs=(every, P(), P(), P(bn, None)),
        check_vma=False,
    )
```

```python
import functools

import jax
import jax.numpy as jnp
from jax import lax
from jax.experimental import pallas as pl
from jax.experimental.pallas import tpu as pltpu
from jax.sharding import Mesh, PartitionSpec as P

epsilon = 1e-05
weight_decay = 5e-05
momentum = 0.9
f32, bf16 = jnp.float32, jnp.bfloat16
rep = ("z", "x")
bn = ("y", "c")
lanes = 128
chunk = 512
groups = chunk // lanes


def swap(value):
    return lax.ppermute(value, "c", [(0, 1), (1, 0)])


def exchange(pieces, axis):
    return lax.all_to_all(pieces, axis, 0, 0, tiled=True)


def copies(value, axis):
    n = lax.axis_size(axis)
    return exchange(jnp.broadcast_to(value[None], (n, *value.shape)), axis)


def fold(row):
    return [row[:, q * lanes : (q + 1) * lanes] for q in range(groups)]


def unfold(tile):
    return jnp.concatenate([tile[q : q + 1] for q in range(groups)], axis=1)


def high_low(value):
    high = value.astype(bf16).astype(f32)
    return high, value - high


def columns(width):
    return [pl.ds(start, chunk) for start in range(0, width, chunk)]


def moments_kernel(acts, own, other, weight, conv, moments):
    core = lax.axis_index("c")
    count, part, cout = own.shape
    for y in range(count):
        at = pl.multiple_of((2 * y + core) * part, part)
        weight[pl.ds(at, part), :] = own[y]
        at = pl.multiple_of((2 * y + 1 - core) * part, part)
        weight[pl.ds(at, part), :] = other[y]
    for j, cols in enumerate(columns(cout)):
        out = jnp.dot(acts[...], weight[:, cols], preferred_element_type=f32)
        conv[:, cols] = out
        mean = jnp.sum(out, axis=0, keepdims=True) / out.shape[0]
        spread = out - mean
        square = jnp.sum(spread * spread, axis=0, keepdims=True)
        tile = jnp.concatenate(fold(mean) + fold(square), axis=0)
        moments[:, 8 * j : 8 * j + 8] = jnp.broadcast_to(tile[None], (moments.shape[0], 8, lanes))


def pooled(moments, rows):
    members = moments.shape[0]
    means, squares = moments[:, :groups], moments[:, groups:]
    mean = jnp.sum(means, axis=0) / members
    offset = means - mean[None]
    square = jnp.sum(squares, axis=0) + rows * jnp.sum(offset * offset, axis=0)
    inv_std = lax.rsqrt(square / (rows * members) + epsilon)
    return unfold(mean), unfold(inv_std)


def stats_kernel(conv, moments, gain, shift, block_input, out_grad, grad, stats):
    rows, cout = conv.shape
    for j, cols in enumerate(columns(cout)):
        mean, inv_std = pooled(moments[:, 8 * j : 8 * j + 8], rows)
        centered = conv[:, cols] - mean
        scale = gain[:, cols] * inv_std
        summed = centered * scale + shift[:, cols] + block_input[:, cols].astype(f32)
        value = jnp.where(summed > 0.0, out_grad[:, cols].astype(f32), 0.0)
        grad[:, cols] = value.astype(bf16)
        sum_grad = jnp.sum(value, axis=0, keepdims=True)
        sum_cross = jnp.sum(value * centered, axis=0, keepdims=True) * inv_std
        tile = jnp.concatenate(fold(sum_grad) + fold(sum_cross), axis=0)
        stats[:, 8 * j : 8 * j + 8] = jnp.broadcast_to(tile[None], (stats.shape[0], 8, lanes))


def weight_kernel(
    conv, moments, stats, gain, grad, acts, grad_conv, mine, theirs, tail, wide, acts_t
):
    core = lax.axis_index("c")
    rows, cout = conv.shape
    group_rows = rows * moments.shape[0]
    nz, nx, length, _ = mine.shape
    part = 8 * nx
    ny = wide.shape[0] // (2 * part)
    halves = cout // nz // lanes
    per = chunk // lanes // halves
    acts_t[...] = acts[...].T
    for j, cols in enumerate(columns(cout)):
        mean, inv_std = pooled(moments[:, 8 * j : 8 * j + 8], rows)
        sums = jnp.sum(stats[:, 8 * j : 8 * j + 8], axis=0)
        sum_grad, sum_cross = sums[:groups], sums[groups:]
        shift = unfold(sum_grad) / group_rows
        slope = inv_std * unfold(sum_cross) / group_rows
        value = grad[:, cols].astype(f32) - shift - (conv[:, cols] - mean) * slope
        narrow = (gain[:, cols] * inv_std * value).astype(bf16)
        grad_conv[:, cols] = narrow
        wide[...] = jnp.dot(acts_t[...], narrow, preferred_element_type=f32)
        planes = (*high_low(sum_grad), *high_low(sum_cross))
        for k in range(per):
            for x in range(nx):
                for out, owner in ((mine, core), (theirs, 1 - core)):
                    rows_of = [
                        wide[
                            pl.ds(pl.multiple_of((2 * y + owner) * part + 8 * x, 8), 8),
                            pl.ds((k * halves + h) * lanes, lanes),
                        ]
                        for h in range(halves)
                        for y in range(ny)
                    ]
                    out[j * per + k, x] = jnp.concatenate(rows_of, axis=0).astype(bf16)
                rows_of = planes[x][k * halves : (k + 1) * halves]
                rows_of = [rows_of, jnp.zeros((16 - halves, lanes), f32)]
                tail[j * per + k, x] = jnp.concatenate(rows_of, axis=0).astype(bf16)


def act_kernel(grad_conv, weight, act_grad, squares):
    act_grad[...] = lax.dot_general(
        grad_conv[...], weight[...], (((1,), (1,)), ((), ())), preferred_element_type=f32
    ).astype(bf16)
    total = jnp.zeros((8, lanes), f32)
    for cols in columns(weight.shape[1]):
        wide = weight[:, cols].astype(f32)
        total += sum(fold(jnp.sum((wide * wide).reshape(-1, 8, chunk), axis=0)))
    squares[...] = total


def total_kernel(partial, summed, out, total):
    ny, length, _ = partial.shape
    halves = length // (8 * ny)
    total[...] = jnp.sum(partial[...].astype(f32), axis=0)
    value = total[...]
    square = jnp.sum(jnp.sum(value * value, axis=0, keepdims=True), axis=1, keepdims=True)
    square = jnp.broadcast_to(square, (1, lanes))
    y = lax.axis_index("y")
    own = [total[pl.ds(pl.multiple_of((h * ny + y) * 8, 8), 8), :] for h in range(halves)]
    extra = [*high_low(summed[length : length + halves, :]), *high_low(square)]
    used = sum(e.shape[0] for e in extra)
    extra.append(jnp.zeros((8 - used, lanes), f32))
    tile = jnp.concatenate(own + extra, axis=0).astype(bf16)
    out[...] = jnp.broadcast_to(tile[None], out.shape)


def step_kernel(nx, parts, squares, weight_squares, weight, velocity, out, gain, shift):
    nz = parts.shape[0] // nx
    halves = out.shape[1] // nz // lanes
    grad_square = jnp.sum(squares[...], axis=0, keepdims=True)[:, :1]
    weight_square = jnp.sum(weight_squares[...], axis=0, keepdims=True)
    weight_square = jnp.sum(weight_square, axis=1, keepdims=True)
    weight_norm = jnp.sqrt(weight_square)
    ratio = weight_norm / (jnp.sqrt(grad_square) + weight_decay * weight_norm)
    at = 8 * halves
    for z in range(nz):
        values = [parts[z * nx + x].astype(f32) for x in range(nx)]
        for h in range(halves):
            cols = pl.ds((z * halves + h) * lanes, lanes)
            weight_grad = jnp.concatenate([v[8 * h : 8 * h + 8] for v in values], axis=0)
            decayed = weight_grad + weight_decay * weight[:, cols].astype(f32)
            out[:, cols] = momentum * velocity[:, cols] + ratio * decayed
            sums = [v[at + h : at + h + 1] + v[at + halves + h : at + halves + h + 1] for v in values]
            shift[:, cols] = sums[0] + sums[1]
            gain[:, cols] = sums[2] + sums[3]


def shape(dims, dtype):
    return jax.ShapeDtypeStruct(dims, dtype)


def whole(dims):
    return pl.BlockSpec(dims, lambda j: (0,) * len(dims))


def params(mib=24):
    return pltpu.CompilerParams(vmem_limit_bytes=mib << 20)


def local(block_input, activations, conv_weight, bn_gain, bn_shift, out_grad, velocity):
    rows, cin = activations.shape
    part, cout = conv_weight.shape
    nz, nx, ny = lax.axis_size("z"), lax.axis_size("x"), lax.axis_size("y")
    members = lax.axis_size(bn)
    gain, shift = bn_gain.reshape(1, cout), bn_shift.reshape(1, cout)
    halves = cout // nz // lanes
    length = halves * ny * 8

    own = copies(conv_weight, "y").reshape(ny, part, cout)
    other = swap(own)
    sums = (members, 2 * cout // lanes, lanes)
    weight, conv, moments = pl.pallas_call(
        moments_kernel,
        grid=(1,),
        in_specs=[whole((rows, cin)), whole((ny, part, cout)), whole((ny, part, cout))],
        out_specs=[whole((cin, cout)), whole((rows, cout)), whole(sums)],
        out_shape=[shape((cin, cout), bf16), shape((rows, cout), f32), shape(sums, f32)],
        compiler_params=params(),
        name="moments",
    )(activations, own, other)
    moments = exchange(moments, bn)

    grad, stats = pl.pallas_call(
        stats_kernel,
        grid=(1,),
        in_specs=[whole((rows, cout)), whole(sums)]
        + [whole((1, cout))] * 2
        + [whole((rows, cout))] * 2,
        out_specs=[whole((rows, cout)), whole(sums)],
        out_shape=[shape((rows, cout), bf16), shape(sums, f32)],
        compiler_params=params(),
        name="stats",
    )(conv, moments, gain, shift, block_input, out_grad)
    stats = exchange(stats, bn)

    piece, extra = (nz, nx, length, lanes), (nz, nx, 16, lanes)
    grad_conv, mine, theirs, tail = pl.pallas_call(
        weight_kernel,
        grid=(1,),
        in_specs=[
            whole((rows, cout)),
            whole(sums),
            whole(sums),
            whole((1, cout)),
            whole((rows, cout)),
            whole((rows, cin)),
        ],
        out_specs=[whole((rows, cout)), whole(piece), whole(piece), whole(extra)],
        out_shape=[
            shape((rows, cout), bf16),
            shape(piece, bf16),
            shape(piece, bf16),
            shape(extra, bf16),
        ],
        scratch_shapes=[
            pltpu.VMEM((cin, chunk), f32),
            pltpu.VMEM((cin, rows), bf16),
        ],
        compiler_params=params(),
        name="weight_partial",
    )(conv, moments, stats, gain, grad, activations)
    arrived = swap(theirs)
    act_grad, squares = pl.pallas_call(
        act_kernel,
        grid=(1,),
        in_specs=[whole((rows, cout)), whole((cin, cout))],
        out_specs=[whole((rows, cin)), whole((8, lanes))],
        out_shape=[shape((rows, cin), bf16), shape((8, lanes), f32)],
        compiler_params=params(),
        cost_estimate=pl.CostEstimate(
            flops=2 * rows * cin * cout, bytes_accessed=2 * (rows + cin) * cout, transcendentals=0
        ),
        name="act_grad",
    )(grad_conv, weight)
    arrived, act_grad = lax.optimization_barrier((arrived, act_grad))
    pair = (mine.astype(f32) + arrived.astype(f32)).astype(bf16)
    pair = jnp.concatenate([pair, tail], axis=2).reshape(nz * nx, length + 16, lanes)
    received = exchange(pair, rep)
    summed = jnp.sum(received.astype(f32), axis=0)
    blocks = copies(summed[:length].astype(bf16), "y")
    blocks = blocks.reshape(ny, length, lanes)
    depth = halves * 8 + 8
    ready = pl.pallas_call(
        total_kernel,
        grid=(1,),
        in_specs=[whole((ny, length, lanes)), whole((length + 16, lanes))],
        out_specs=whole((nz * nx, depth, lanes)),
        out_shape=shape((nz * nx, depth, lanes), bf16),
        scratch_shapes=[pltpu.VMEM((length, lanes), f32)],
        compiler_params=params(),
        name="totals",
    )(blocks, summed)
    ready = exchange(ready, rep)
    at = halves * 8 + 2 * halves
    square = jnp.sum(ready[:, at : at + 2].astype(f32), axis=(0, 1))
    square = lax.all_gather(square, "c")
    new_velocity, gain_grad, shift_grad = pl.pallas_call(
        functools.partial(step_kernel, nx),
        grid=(1,),
        in_specs=[
            whole((nz * nx, depth, lanes)),
            whole((2, lanes)),
            whole((8, lanes)),
            whole((part, cout)),
            whole((part, cout)),
        ],
        out_specs=[whole((part, cout)), whole((1, cout)), whole((1, cout))],
        out_shape=[shape((part, cout), f32), shape((1, cout), f32), shape((1, cout), f32)],
        compiler_params=params(),
        name="step",
    )(ready, square, squares, conv_weight, velocity)
    return (act_grad, gain_grad.reshape(cout), shift_grad.reshape(cout), new_velocity)


def solution(mesh, dims=(8, 4, 8, 2)):
    fine = Mesh(mesh.devices.reshape(dims), ("z", "x", "y", "c"))
    every = P(("z", "x", "y", "c"), None)
    return jax.shard_map(
        local,
        mesh=fine,
        in_specs=(every, every, P(bn, None), P(), P(), every, P(bn, None)),
        out_specs=(every, P(), P(), P(bn, None)),
        check_vma=False,
    )
```

```python
import functools

import jax
import jax.numpy as jnp
from jax import lax
from jax.experimental import pallas as pl
from jax.experimental.pallas import tpu as pltpu
from jax.sharding import Mesh, PartitionSpec as P

epsilon = 1e-05
weight_decay = 5e-05
momentum = 0.9
f32, bf16 = jnp.float32, jnp.bfloat16
rep = ("z", "x")
bn = ("y", "c")
lanes = 128
chunk = 512
groups = chunk // lanes


def swap(value):
    return lax.ppermute(value, "c", [(0, 1), (1, 0)])


def exchange(pieces, axis):
    return lax.all_to_all(pieces, axis, 0, 0, tiled=True)


def copies(value, axis):
    n = lax.axis_size(axis)
    return exchange(jnp.broadcast_to(value[None], (n, *value.shape)), axis)


def fold(row):
    return [row[:, q * lanes : (q + 1) * lanes] for q in range(groups)]


def unfold(tile):
    return jnp.concatenate([tile[q : q + 1] for q in range(groups)], axis=1)


def high_low(value):
    high = value.astype(bf16).astype(f32)
    return high, value - high


def columns(width):
    return [pl.ds(start, chunk) for start in range(0, width, chunk)]


def moments_kernel(acts, own, other, weight, conv, moments):
    core = lax.axis_index("c")
    count, part, cout = own.shape
    for y in range(count):
        at = pl.multiple_of((2 * y + core) * part, part)
        weight[pl.ds(at, part), :] = own[y]
        at = pl.multiple_of((2 * y + 1 - core) * part, part)
        weight[pl.ds(at, part), :] = other[y]
    for j, cols in enumerate(columns(cout)):
        out = jnp.dot(acts[...], weight[:, cols], preferred_element_type=f32)
        conv[:, cols] = out
        mean = jnp.sum(out, axis=0, keepdims=True) / out.shape[0]
        spread = out - mean
        square = jnp.sum(spread * spread, axis=0, keepdims=True)
        tile = jnp.concatenate(fold(mean) + fold(square), axis=0)
        moments[:, 8 * j : 8 * j + 8] = jnp.broadcast_to(tile[None], (moments.shape[0], 8, lanes))


def pooled(moments, rows):
    members = moments.shape[0]
    means, squares = moments[:, :groups], moments[:, groups:]
    mean = jnp.sum(means, axis=0) / members
    offset = means - mean[None]
    square = jnp.sum(squares, axis=0) + rows * jnp.sum(offset * offset, axis=0)
    inv_std = lax.rsqrt(square / (rows * members) + epsilon)
    return unfold(mean), unfold(inv_std)


def stats_kernel(conv, moments, gain, shift, block_input, out_grad, grad, stats):
    rows, cout = conv.shape
    tiles = []
    for j, cols in enumerate(columns(cout)):
        mean, inv_std = pooled(moments[:, 8 * j : 8 * j + 8], rows)
        centered = conv[:, cols] - mean
        scale = gain[:, cols] * inv_std
        summed = centered * scale + shift[:, cols] + block_input[:, cols].astype(f32)
        value = jnp.where(summed > 0.0, out_grad[:, cols].astype(f32), 0.0)
        grad[:, cols] = value.astype(bf16)
        sum_grad = jnp.sum(value, axis=0, keepdims=True)
        sum_cross = jnp.sum(value * centered, axis=0, keepdims=True) * inv_std
        tiles += fold(sum_grad) + fold(sum_cross)
    tile = jnp.concatenate(tiles, axis=0).astype(bf16)
    stats[...] = jnp.broadcast_to(tile[None], stats.shape)


def weight_kernel(
    conv, moments, stats, gain, grad, acts, grad_conv, mine, theirs, tail, wide, acts_t
):
    core = lax.axis_index("c")
    rows, cout = conv.shape
    group_rows = rows * moments.shape[0]
    nz, nx, length, _ = mine.shape
    part = 8 * nx
    ny = wide.shape[0] // (2 * part)
    halves = cout // nz // lanes
    per = chunk // lanes // halves
    acts_t[...] = acts[...].T
    totals = jnp.sum(stats[...].astype(f32), axis=0)
    for j, cols in enumerate(columns(cout)):
        mean, inv_std = pooled(moments[:, 8 * j : 8 * j + 8], rows)
        sums = totals[8 * j : 8 * j + 8]
        sum_grad, sum_cross = sums[:groups], sums[groups:]
        shift = unfold(sum_grad) / group_rows
        slope = inv_std * unfold(sum_cross) / group_rows
        value = grad[:, cols].astype(f32) - shift - (conv[:, cols] - mean) * slope
        narrow = (gain[:, cols] * inv_std * value).astype(bf16)
        grad_conv[:, cols] = narrow
        wide[...] = jnp.dot(acts_t[...], narrow, preferred_element_type=f32)
        planes = (*high_low(sum_grad), *high_low(sum_cross))
        for k in range(per):
            for x in range(nx):
                for out, owner in ((mine, core), (theirs, 1 - core)):
                    rows_of = [
                        wide[
                            pl.ds(pl.multiple_of((2 * y + owner) * part + 8 * x, 8), 8),
                            pl.ds((k * halves + h) * lanes, lanes),
                        ]
                        for h in range(halves)
                        for y in range(ny)
                    ]
                    out[j * per + k, x] = jnp.concatenate(rows_of, axis=0).astype(bf16)
                rows_of = planes[x][k * halves : (k + 1) * halves]
                rows_of = [rows_of, jnp.zeros((8 - halves, lanes), f32)]
                tail[j * per + k, x] = jnp.concatenate(rows_of, axis=0)


def act_kernel(grad_conv, weight, act_grad, squares):
    act_grad[...] = lax.dot_general(
        grad_conv[...], weight[...], (((1,), (1,)), ((), ())), preferred_element_type=f32
    ).astype(bf16)
    total = jnp.zeros((8, lanes), f32)
    for cols in columns(weight.shape[1]):
        wide = weight[:, cols].astype(f32)
        total += sum(fold(jnp.sum((wide * wide).reshape(-1, 8, chunk), axis=0)))
    squares[...] = total


def total_kernel(partial, summed, out, total):
    ny, length, _ = partial.shape
    halves = length // (8 * ny)
    total[...] = jnp.sum(partial[...].astype(f32), axis=0)
    value = total[...]
    square = jnp.sum(jnp.sum(value * value, axis=0, keepdims=True), axis=1, keepdims=True)
    square = jnp.broadcast_to(square, (1, lanes))
    y = lax.axis_index("y")
    own = [total[pl.ds(pl.multiple_of((h * ny + y) * 8, 8), 8), :] for h in range(halves)]
    extra = [*high_low(summed[length : length + halves, :]), *high_low(square)]
    used = sum(e.shape[0] for e in extra)
    extra.append(jnp.zeros((8 - used, lanes), f32))
    tile = jnp.concatenate(own + extra, axis=0).astype(bf16)
    out[...] = jnp.broadcast_to(tile[None], out.shape)


def step_kernel(nx, parts, squares, weight_squares, weight, velocity, out, gain, shift):
    nz = parts.shape[0] // nx
    halves = out.shape[1] // nz // lanes
    grad_square = jnp.sum(squares[...], axis=0, keepdims=True)[:, :1]
    weight_square = jnp.sum(weight_squares[...], axis=0, keepdims=True)
    weight_square = jnp.sum(weight_square, axis=1, keepdims=True)
    weight_norm = jnp.sqrt(weight_square)
    ratio = weight_norm / (jnp.sqrt(grad_square) + weight_decay * weight_norm)
    at = 8 * halves
    for z in range(nz):
        values = [parts[z * nx + x].astype(f32) for x in range(nx)]
        for h in range(halves):
            cols = pl.ds((z * halves + h) * lanes, lanes)
            weight_grad = jnp.concatenate([v[8 * h : 8 * h + 8] for v in values], axis=0)
            decayed = weight_grad + weight_decay * weight[:, cols].astype(f32)
            out[:, cols] = momentum * velocity[:, cols] + ratio * decayed
            sums = [v[at + h : at + h + 1] + v[at + halves + h : at + halves + h + 1] for v in values]
            shift[:, cols] = sums[0] + sums[1]
            gain[:, cols] = sums[2] + sums[3]


def shape(dims, dtype):
    return jax.ShapeDtypeStruct(dims, dtype)


def whole(dims):
    return pl.BlockSpec(dims, lambda j: (0,) * len(dims))


def params(mib=24):
    return pltpu.CompilerParams(vmem_limit_bytes=mib << 20)


def local(block_input, activations, conv_weight, bn_gain, bn_shift, out_grad, velocity):
    rows, cin = activations.shape
    part, cout = conv_weight.shape
    nz, nx, ny = lax.axis_size("z"), lax.axis_size("x"), lax.axis_size("y")
    members = lax.axis_size(bn)
    gain, shift = bn_gain.reshape(1, cout), bn_shift.reshape(1, cout)
    halves = cout // nz // lanes
    length = halves * ny * 8

    own = copies(conv_weight, "y").reshape(ny, part, cout)
    other = swap(own)
    sums = (members, 2 * cout // lanes, lanes)
    weight, conv, moments = pl.pallas_call(
        moments_kernel,
        grid=(1,),
        in_specs=[whole((rows, cin)), whole((ny, part, cout)), whole((ny, part, cout))],
        out_specs=[whole((cin, cout)), whole((rows, cout)), whole(sums)],
        out_shape=[shape((cin, cout), bf16), shape((rows, cout), f32), shape(sums, f32)],
        compiler_params=params(),
        name="moments",
    )(activations, own, other)
    moments = exchange(moments, bn)

    grad, stats = pl.pallas_call(
        stats_kernel,
        grid=(1,),
        in_specs=[whole((rows, cout)), whole(sums)]
        + [whole((1, cout))] * 2
        + [whole((rows, cout))] * 2,
        out_specs=[whole((rows, cout)), whole(sums)],
        out_shape=[shape((rows, cout), bf16), shape(sums, bf16)],
        compiler_params=params(),
        name="stats",
    )(conv, moments, gain, shift, block_input, out_grad)
    stats = exchange(stats, bn)

    piece, extra = (nz, nx, length, lanes), (nz, nx, 8, lanes)
    grad_conv, mine, theirs, tail = pl.pallas_call(
        weight_kernel,
        grid=(1,),
        in_specs=[
            whole((rows, cout)),
            whole(sums),
            whole(sums),
            whole((1, cout)),
            whole((rows, cout)),
            whole((rows, cin)),
        ],
        out_specs=[whole((rows, cout)), whole(piece), whole(piece), whole(extra)],
        out_shape=[
            shape((rows, cout), bf16),
            shape(piece, bf16),
            shape(piece, bf16),
            shape(extra, f32),
        ],
        scratch_shapes=[
            pltpu.VMEM((cin, chunk), f32),
            pltpu.VMEM((cin, rows), bf16),
        ],
        compiler_params=params(),
        name="weight_partial",
    )(conv, moments, stats, gain, grad, activations)
    arrived = swap(theirs)
    act_grad, squares = pl.pallas_call(
        act_kernel,
        grid=(1,),
        in_specs=[whole((rows, cout)), whole((cin, cout))],
        out_specs=[whole((rows, cin)), whole((8, lanes))],
        out_shape=[shape((rows, cin), bf16), shape((8, lanes), f32)],
        compiler_params=params(),
        cost_estimate=pl.CostEstimate(
            flops=2 * rows * cin * cout, bytes_accessed=2 * (rows + cin) * cout, transcendentals=0
        ),
        name="act_grad",
    )(grad_conv, weight)
    arrived, act_grad = lax.optimization_barrier((arrived, act_grad))
    pair = (mine.astype(f32) + arrived.astype(f32)).astype(bf16)
    pair = jnp.concatenate([pair, tail.astype(bf16)], axis=2).reshape(nz * nx, length + 8, lanes)
    received = exchange(pair, rep)
    summed = jnp.sum(received.astype(f32), axis=0)
    blocks = copies(summed[:length].astype(bf16), "y")
    blocks = blocks.reshape(ny, length, lanes)
    depth = halves * 8 + 8
    ready = pl.pallas_call(
        total_kernel,
        grid=(1,),
        in_specs=[whole((ny, length, lanes)), whole((length + 8, lanes))],
        out_specs=whole((nz * nx, depth, lanes)),
        out_shape=shape((nz * nx, depth, lanes), bf16),
        scratch_shapes=[pltpu.VMEM((length, lanes), f32)],
        compiler_params=params(),
        name="totals",
    )(blocks, summed)
    ready = exchange(ready, rep)
    at = halves * 8 + 2 * halves
    square = jnp.sum(ready[:, at : at + 2].astype(f32), axis=(0, 1))
    square = lax.all_gather(square, "c")
    new_velocity, gain_grad, shift_grad = pl.pallas_call(
        functools.partial(step_kernel, nx),
        grid=(1,),
        in_specs=[
            whole((nz * nx, depth, lanes)),
            whole((2, lanes)),
            whole((8, lanes)),
            whole((part, cout)),
            whole((part, cout)),
        ],
        out_specs=[whole((part, cout)), whole((1, cout)), whole((1, cout))],
        out_shape=[shape((part, cout), f32), shape((1, cout), f32), shape((1, cout), f32)],
        compiler_params=params(),
        name="step",
    )(ready, square, squares, conv_weight, velocity)
    return (act_grad, gain_grad.reshape(cout), shift_grad.reshape(cout), new_velocity)


def solution(mesh, dims=(8, 4, 8, 2)):
    fine = Mesh(mesh.devices.reshape(dims), ("z", "x", "y", "c"))
    every = P(("z", "x", "y", "c"), None)
    return jax.shard_map(
        local,
        mesh=fine,
        in_specs=(every, every, P(bn, None), P(), P(), every, P(bn, None)),
        out_specs=(every, P(), P(), P(bn, None)),
        check_vma=False,
    )
```

```python
import functools

import jax
import jax.numpy as jnp
from jax import lax
from jax.experimental import pallas as pl
from jax.experimental.pallas import tpu as pltpu
from jax.sharding import Mesh, PartitionSpec as P

epsilon = 1e-05
weight_decay = 5e-05
momentum = 0.9
f32, bf16 = jnp.float32, jnp.bfloat16
rep = ("zh", "zl", "x")
y_axes = ("yh", "yl")
bn = ("yh", "yl", "c")
near = ("zl", "x", "yl")
far = ("zh", "yh")
lanes = 128
chunk = 512
groups = chunk // lanes


def swap(value):
    return lax.ppermute(value, "c", [(0, 1), (1, 0)])


def exchange(pieces, axis):
    return lax.all_to_all(pieces, axis, 0, 0, tiled=True)


def copies(value, axis):
    n = lax.axis_size(axis)
    return exchange(jnp.broadcast_to(value[None], (n, *value.shape)), axis)


def fold(row):
    return [row[:, q * lanes : (q + 1) * lanes] for q in range(groups)]


def unfold(tile):
    return jnp.concatenate([tile[q : q + 1] for q in range(groups)], axis=1)


def high_low(value):
    high = value.astype(bf16).astype(f32)
    return high, value - high


def columns(width):
    return [pl.ds(start, chunk) for start in range(0, width, chunk)]


def moments_kernel(acts, own, other, weight, conv, moments):
    core = lax.axis_index("c")
    count, part, cout = own.shape
    for y in range(count):
        at = pl.multiple_of((2 * y + core) * part, part)
        weight[pl.ds(at, part), :] = own[y]
        at = pl.multiple_of((2 * y + 1 - core) * part, part)
        weight[pl.ds(at, part), :] = other[y]
    for j, cols in enumerate(columns(cout)):
        out = jnp.dot(acts[...], weight[:, cols], preferred_element_type=f32)
        conv[:, cols] = out
        mean = jnp.sum(out, axis=0, keepdims=True) / out.shape[0]
        spread = out - mean
        square = jnp.sum(spread * spread, axis=0, keepdims=True)
        tile = jnp.concatenate(fold(mean) + fold(square), axis=0)
        moments[:, 8 * j : 8 * j + 8] = jnp.broadcast_to(tile[None], (moments.shape[0], 8, lanes))


def pooled(moments, rows):
    members = moments.shape[0]
    means, squares = moments[:, :groups], moments[:, groups:]
    mean = jnp.sum(means, axis=0) / members
    offset = means - mean[None]
    square = jnp.sum(squares, axis=0) + rows * jnp.sum(offset * offset, axis=0)
    inv_std = lax.rsqrt(square / (rows * members) + epsilon)
    return unfold(mean), unfold(inv_std)


def stats_kernel(conv, moments, gain, shift, block_input, out_grad, grad, stats):
    rows, cout = conv.shape
    tiles = []
    for j, cols in enumerate(columns(cout)):
        mean, inv_std = pooled(moments[:, 8 * j : 8 * j + 8], rows)
        centered = conv[:, cols] - mean
        scale = gain[:, cols] * inv_std
        summed = centered * scale + shift[:, cols] + block_input[:, cols].astype(f32)
        value = jnp.where(summed > 0.0, out_grad[:, cols].astype(f32), 0.0)
        grad[:, cols] = value.astype(bf16)
        sum_grad = jnp.sum(value, axis=0, keepdims=True)
        sum_cross = jnp.sum(value * centered, axis=0, keepdims=True) * inv_std
        tiles += fold(sum_grad) + fold(sum_cross)
    tile = jnp.concatenate(tiles, axis=0).astype(bf16)
    stats[...] = jnp.broadcast_to(tile[None], stats.shape)


def weight_kernel(
    sizes, conv, moments, stats, gain, grad, acts, grad_conv, mine, theirs, tail, wide, acts_t
):
    nzl, nx, nyl, nyh = sizes
    core = lax.axis_index("c")
    rows, cout = conv.shape
    group_rows = rows * moments.shape[0]
    part = 8 * nx
    acts_t[...] = acts[...].T
    totals = jnp.sum(stats[...].astype(f32), axis=0)
    per = cout // nzl // chunk
    for j, cols in enumerate(columns(cout)):
        mean, inv_std = pooled(moments[:, 8 * j : 8 * j + 8], rows)
        sums = totals[8 * j : 8 * j + 8]
        sum_grad, sum_cross = sums[:groups], sums[groups:]
        shift = unfold(sum_grad) / group_rows
        slope = inv_std * unfold(sum_cross) / group_rows
        value = grad[:, cols].astype(f32) - shift - (conv[:, cols] - mean) * slope
        narrow = (gain[:, cols] * inv_std * value).astype(bf16)
        grad_conv[:, cols] = narrow
        wide[...] = jnp.dot(acts_t[...], narrow, preferred_element_type=f32)
        planes = (*high_low(sum_grad), *high_low(sum_cross))
        zl, k = j // per, j % per
        length = groups * nyh * 8
        for x in range(nx):
            for yl in range(nyl):
                piece = (zl * nx + x) * nyl + yl
                for out, owner in ((mine, core), (theirs, 1 - core)):
                    rows_of = [
                        wide[
                            pl.ds(pl.multiple_of((2 * (yh * nyl + yl) + owner) * part + 8 * x, 8), 8),
                            pl.ds(q * lanes, lanes),
                        ]
                        for q in range(groups)
                        for yh in range(nyh)
                    ]
                    rows_of = jnp.concatenate(rows_of, axis=0).astype(bf16)
                    out[piece, k * length : (k + 1) * length] = rows_of
                tail[piece, k * groups : (k + 1) * groups] = planes[x] / (nyl * nyh)


def act_kernel(grad_conv, weight, act_grad, squares):
    act_grad[...] = lax.dot_general(
        grad_conv[...], weight[...], (((1,), (1,)), ((), ())), preferred_element_type=f32
    ).astype(bf16)
    total = jnp.zeros((8, lanes), f32)
    for cols in columns(weight.shape[1]):
        wide = weight[:, cols].astype(f32)
        total += sum(fold(jnp.sum((wide * wide).reshape(-1, 8, chunk), axis=0)))
    squares[...] = total


def near_kernel(nyh, received, out, total):
    count, depth, _ = out.shape
    nzh = count // nyh
    total[...] = jnp.sum(received[...].astype(f32), axis=0)
    halves = (total.shape[0] - 8) // (nzh * nyh * 8)
    base = nzh * halves * nyh * 8
    for zh in range(nzh):
        high, low = high_low(total[base + zh * halves : base + (zh + 1) * halves, :])
        extra = jnp.concatenate([high, low, jnp.zeros((8 - 2 * halves, lanes), f32)], axis=0)
        for yh in range(nyh):
            starts = [((zh * halves + h) * nyh + yh) * 8 for h in range(halves)]
            own = [total[at : at + 8, :] for at in starts]
            out[zh * nyh + yh] = jnp.concatenate([*own, extra], axis=0).astype(bf16)


def far_kernel(halves, received, out):
    total = jnp.sum(received[...].astype(f32), axis=0)
    at = 8 * halves
    value = total[:at]
    square = jnp.sum(jnp.sum(value * value, axis=0, keepdims=True), axis=1, keepdims=True)
    square = jnp.broadcast_to(square, (1, lanes))
    tail = total[at : at + halves] + total[at + halves : at + 2 * halves]
    extra = [*high_low(tail), *high_low(square)]
    used = sum(e.shape[0] for e in extra)
    extra.append(jnp.zeros((8 - used, lanes), f32))
    tile = jnp.concatenate([value, *extra], axis=0).astype(bf16)
    out[...] = jnp.broadcast_to(tile[None], out.shape)


def step_kernel(nzl, nx, parts, squares, weight_squares, weight, velocity, out, gain, shift):
    nz = parts.shape[0] // nx
    nzh = nz // nzl
    halves = out.shape[1] // nz // lanes
    grad_square = jnp.sum(squares[...], axis=0)[:1, :1]
    weight_square = jnp.sum(weight_squares[...], axis=0, keepdims=True)
    weight_square = jnp.sum(weight_square, axis=1, keepdims=True)
    weight_norm = jnp.sqrt(weight_square)
    ratio = weight_norm / (jnp.sqrt(grad_square) + weight_decay * weight_norm)
    at = 8 * halves
    for z in range(nz):
        values = [parts[z * nx + x].astype(f32) for x in range(nx)]
        for h in range(halves):
            cols = pl.ds(((z % nzl * nzh + z // nzl) * halves + h) * lanes, lanes)
            weight_grad = jnp.concatenate([v[8 * h : 8 * h + 8] for v in values], axis=0)
            decayed = weight_grad + weight_decay * weight[:, cols].astype(f32)
            out[:, cols] = momentum * velocity[:, cols] + ratio * decayed
            sums = [v[at + h : at + h + 1] + v[at + halves + h : at + halves + h + 1] for v in values]
            shift[:, cols] = sums[0] + sums[1]
            gain[:, cols] = sums[2] + sums[3]


def shape(dims, dtype):
    return jax.ShapeDtypeStruct(dims, dtype)


def whole(dims):
    return pl.BlockSpec(dims, lambda j: (0,) * len(dims))


def params(mib=24):
    return pltpu.CompilerParams(vmem_limit_bytes=mib << 20)


def local(block_input, activations, conv_weight, bn_gain, bn_shift, out_grad, velocity):
    rows, cin = activations.shape
    part, cout = conv_weight.shape
    nzh, nzl, nx = (lax.axis_size(a) for a in rep)
    nyh, nyl = (lax.axis_size(a) for a in y_axes)
    nz, ny = nzh * nzl, nyh * nyl
    members = lax.axis_size(bn)
    gain, shift = bn_gain.reshape(1, cout), bn_shift.reshape(1, cout)
    halves = cout // nz // lanes
    length = nzh * halves * nyh * 8
    depth = halves * 8 + 8

    own = copies(conv_weight, y_axes).reshape(ny, part, cout)
    other = swap(own)
    sums = (members, 2 * cout // lanes, lanes)
    weight, conv, moments = pl.pallas_call(
        moments_kernel,
        grid=(1,),
        in_specs=[whole((rows, cin)), whole((ny, part, cout)), whole((ny, part, cout))],
        out_specs=[whole((cin, cout)), whole((rows, cout)), whole(sums)],
        out_shape=[shape((cin, cout), bf16), shape((rows, cout), f32), shape(sums, f32)],
        compiler_params=params(),
        name="moments",
    )(activations, own, other)
    moments = exchange(moments, bn)

    grad, stats = pl.pallas_call(
        stats_kernel,
        grid=(1,),
        in_specs=[whole((rows, cout)), whole(sums)]
        + [whole((1, cout))] * 2
        + [whole((rows, cout))] * 2,
        out_specs=[whole((rows, cout)), whole(sums)],
        out_shape=[shape((rows, cout), bf16), shape(sums, bf16)],
        compiler_params=params(),
        name="stats",
    )(conv, moments, gain, shift, block_input, out_grad)
    stats = exchange(stats, bn)

    pieces = nzl * nx * nyl
    piece, extra = (pieces, length, lanes), (pieces, 8, lanes)
    grad_conv, mine, theirs, tail = pl.pallas_call(
        functools.partial(weight_kernel, (nzl, nx, nyl, nyh)),
        grid=(1,),
        in_specs=[
            whole((rows, cout)),
            whole(sums),
            whole(sums),
            whole((1, cout)),
            whole((rows, cout)),
            whole((rows, cin)),
        ],
        out_specs=[whole((rows, cout)), whole(piece), whole(piece), whole(extra)],
        out_shape=[
            shape((rows, cout), bf16),
            shape(piece, bf16),
            shape(piece, bf16),
            shape(extra, f32),
        ],
        scratch_shapes=[
            pltpu.VMEM((cin, chunk), f32),
            pltpu.VMEM((cin, rows), bf16),
        ],
        compiler_params=params(),
        name="weight_partial",
    )(conv, moments, stats, gain, grad, activations)
    arrived = swap(theirs)
    act_grad, squares = pl.pallas_call(
        act_kernel,
        grid=(1,),
        in_specs=[whole((rows, cout)), whole((cin, cout))],
        out_specs=[whole((rows, cin)), whole((8, lanes))],
        out_shape=[shape((rows, cin), bf16), shape((8, lanes), f32)],
        compiler_params=params(),
        cost_estimate=pl.CostEstimate(
            flops=2 * rows * cin * cout, bytes_accessed=2 * (rows + cin) * cout, transcendentals=0
        ),
        name="act_grad",
    )(grad_conv, weight)
    arrived, act_grad = lax.optimization_barrier((arrived, act_grad))
    pair = (mine.astype(f32) + arrived.astype(f32)).astype(bf16)
    pair = jnp.concatenate([pair, tail.astype(bf16)], axis=1)
    received = exchange(pair, near)
    partial = pl.pallas_call(
        functools.partial(near_kernel, nyh),
        grid=(1,),
        in_specs=[whole((pieces, length + 8, lanes))],
        out_specs=whole((nzh * nyh, depth, lanes)),
        out_shape=shape((nzh * nyh, depth, lanes), bf16),
        scratch_shapes=[pltpu.VMEM((length + 8, lanes), f32)],
        compiler_params=params(),
        name="near_sum",
    )(received)
    partial = exchange(partial, far)
    ready = pl.pallas_call(
        functools.partial(far_kernel, halves),
        grid=(1,),
        in_specs=[whole((nzh * nyh, depth, lanes))],
        out_specs=whole((nz * nx, depth, lanes)),
        out_shape=shape((nz * nx, depth, lanes), bf16),
        compiler_params=params(),
        name="far_sum",
    )(partial)
    ready = exchange(ready, rep)
    at = halves * 8 + 2 * halves
    square = jnp.sum(ready[:, at : at + 2].astype(f32), axis=(0, 1))
    square = exchange(jnp.broadcast_to(square, (members, 8, lanes)), bn)
    new_velocity, gain_grad, shift_grad = pl.pallas_call(
        functools.partial(step_kernel, nzl, nx),
        grid=(1,),
        in_specs=[
            whole((nz * nx, depth, lanes)),
            whole((members, 8, lanes)),
            whole((8, lanes)),
            whole((part, cout)),
            whole((part, cout)),
        ],
        out_specs=[whole((part, cout)), whole((1, cout)), whole((1, cout))],
        out_shape=[shape((part, cout), f32), shape((1, cout), f32), shape((1, cout), f32)],
        compiler_params=params(),
        name="step",
    )(ready, square, squares, conv_weight, velocity)
    return (act_grad, gain_grad.reshape(cout), shift_grad.reshape(cout), new_velocity)


def solution(mesh, dims=(4, 2, 4, 4, 2, 2)):
    fine = Mesh(mesh.devices.reshape(dims), rep + bn)
    every = P(rep + bn, None)
    return jax.shard_map(
        local,
        mesh=fine,
        in_specs=(every, every, P(bn, None), P(), P(), every, P(bn, None)),
        out_specs=(every, P(), P(), P(bn, None)),
        check_vma=False,
    )
```

```python
import functools

import jax
import jax.numpy as jnp
from jax import lax
from jax.experimental import pallas as pl
from jax.experimental.pallas import tpu as pltpu
from jax.sharding import Mesh, PartitionSpec as P

epsilon = 1e-05
weight_decay = 5e-05
momentum = 0.9
f32, bf16 = jnp.float32, jnp.bfloat16
rep = ("zh", "zl", "x")
y_axes = ("yh", "yl")
bn = ("yh", "yl", "c")
near = ("zl", "x", "yl")
far = ("zh", "yh")
lanes = 128
chunk = 512
groups = chunk // lanes


def swap(value):
    return lax.ppermute(value, "c", [(0, 1), (1, 0)])


def exchange(pieces, axis):
    return lax.all_to_all(pieces, axis, 0, 0, tiled=True)


def copies(value, axis):
    n = lax.axis_size(axis)
    return exchange(jnp.broadcast_to(value[None], (n, *value.shape)), axis)


def fold(row):
    return [row[:, q * lanes : (q + 1) * lanes] for q in range(groups)]


def unfold(tile):
    return jnp.concatenate([tile[q : q + 1] for q in range(groups)], axis=1)


def high_low(value):
    high = value.astype(bf16).astype(f32)
    return high, value - high


def columns(width):
    return [pl.ds(start, chunk) for start in range(0, width, chunk)]


def moments_kernel(acts, acts_other, weight, conv, conv_other, moments):
    count = 2 * conv.shape[0]
    for j, cols in enumerate(columns(conv.shape[1])):
        both = []
        for rows, out in ((acts, conv), (acts_other, conv_other)):
            value = jnp.dot(rows[...], weight[:, cols], preferred_element_type=f32)
            out[:, cols] = value
            both.append(value)
        mean = sum(jnp.sum(value, axis=0, keepdims=True) for value in both) / count
        square = sum(jnp.sum((v - mean) * (v - mean), axis=0, keepdims=True) for v in both)
        tile = jnp.concatenate(fold(mean) + fold(square), axis=0)
        moments[:, 8 * j : 8 * j + 8] = jnp.broadcast_to(tile[None], (moments.shape[0], 8, lanes))


def pooled(moments, rows):
    members = moments.shape[0]
    means, squares = moments[:, :groups], moments[:, groups:]
    mean = jnp.sum(means, axis=0) / members
    offset = means - mean[None]
    square = jnp.sum(squares, axis=0) + rows * jnp.sum(offset * offset, axis=0)
    inv_std = lax.rsqrt(square / (rows * members) + epsilon)
    return unfold(mean), unfold(inv_std)


def stats_kernel(
    conv, conv_other, moments, gain, shift, block, block_other, out, out_other, grad, grad_other, stats
):
    rows, half = conv.shape
    core = lax.axis_index("c")
    for j, cols in enumerate(columns(half)):
        place = pl.ds(pl.multiple_of(core * half + j * chunk, chunk), chunk)
        mean, inv_std = pooled(moments[:, 8 * j : 8 * j + 8], 2 * rows)
        scale, bias = gain[:, place] * inv_std, shift[:, place]
        sum_grad = sum_cross = 0.0
        for of, added, incoming, result in (
            (conv, block[:, place], out[:, place], grad),
            (conv_other, block_other[:, cols], out_other[:, cols], grad_other),
        ):
            centered = of[:, cols] - mean
            summed = centered * scale + bias + added.astype(f32)
            value = jnp.where(summed > 0.0, incoming.astype(f32), 0.0)
            result[:, cols] = value.astype(bf16)
            sum_grad += jnp.sum(value, axis=0, keepdims=True)
            sum_cross += jnp.sum(value * centered, axis=0, keepdims=True)
        tile = jnp.concatenate(fold(sum_grad) + fold(sum_cross * inv_std), axis=0)
        stats[:, 8 * j : 8 * j + 8] = jnp.broadcast_to(tile[None], (stats.shape[0], 8, lanes))


def weight_kernel(
    sizes,
    conv,
    conv_other,
    moments,
    stats,
    gain,
    grad,
    grad_other,
    acts,
    acts_other,
    grad_conv,
    grad_conv_other,
    out,
    wide,
    acts_t,
    acts_t_other,
):
    nx, nyl, nyh = sizes
    core = lax.axis_index("c")
    rows, half = conv.shape
    group_rows = 2 * rows * moments.shape[0]
    part = wide.shape[0] // (nyl * nyh)
    step = part // nx
    length = groups * nyh * step
    acts_t[...] = acts[...].T
    acts_t_other[...] = acts_other[...].T
    for j, cols in enumerate(columns(half)):
        place = pl.ds(pl.multiple_of(core * half + j * chunk, chunk), chunk)
        mean, inv_std = pooled(moments[:, 8 * j : 8 * j + 8], 2 * rows)
        sums = jnp.sum(stats[:, 8 * j : 8 * j + 8], axis=0)
        sum_grad, sum_cross = sums[:groups], sums[groups:]
        shift = unfold(sum_grad) / group_rows
        slope = inv_std * unfold(sum_cross) / group_rows
        scale = gain[:, place] * inv_std
        product = 0.0
        for of, pre, left, result in (
            (conv, grad, acts_t, grad_conv),
            (conv_other, grad_other, acts_t_other, grad_conv_other),
        ):
            value = pre[:, cols].astype(f32) - shift - (of[:, cols] - mean) * slope
            narrow = (scale * value).astype(bf16)
            result[:, cols] = narrow
            product += jnp.dot(left[...], narrow, preferred_element_type=f32)
        wide[...] = product
        planes = (*high_low(sum_grad), *high_low(sum_cross))
        for x in range(nx):
            last = jnp.concatenate(
                [planes[x] / (nyl * nyh), jnp.zeros((16 - groups, lanes), f32)], axis=0
            )
            for yl in range(nyl):
                piece = (j * nx + x) * nyl + yl
                rows_of = [
                    wide[
                        pl.ds((yh * nyl + yl) * part + step * x, step), pl.ds(q * lanes, lanes)
                    ]
                    for q in range(groups)
                    for yh in range(nyh)
                ]
                out[piece, :length] = jnp.concatenate(rows_of, axis=0).astype(bf16)
                out[piece, length:] = last.astype(bf16)


def act_kernel(grad_conv, grad_conv_other, weight, act, act_other, squares):
    dims = (((1,), (1,)), ((), ()))
    act[...] = lax.dot_general(grad_conv[...], weight[...], dims, preferred_element_type=f32)
    act_other[...] = lax.dot_general(
        grad_conv_other[...], weight[...], dims, preferred_element_type=f32
    ).astype(bf16)
    total = jnp.zeros((8, lanes), f32)
    for cols in columns(weight.shape[1]):
        wide = weight[:, cols].astype(f32)
        total += sum(fold(jnp.sum((wide * wide).reshape(-1, 8, chunk), axis=0)))
    squares[...] = total


def near_kernel(nyh, received, out, total):
    count, depth, _ = out.shape
    step = depth - 8
    total[...] = jnp.sum(received[...].astype(f32), axis=0)
    for zh in range(count // nyh):
        base = count * step + zh
        high, low = high_low(total[base : base + 1, :])
        extra = jnp.concatenate([high, low, jnp.zeros((6, lanes), f32)], axis=0)
        for yh in range(nyh):
            at = (zh * nyh + yh) * step
            tile = jnp.concatenate([total[at : at + step, :], extra], axis=0)
            out[zh * nyh + yh] = tile.astype(bf16)


def far_kernel(received, out):
    total = jnp.sum(received[...].astype(f32), axis=0)
    step = total.shape[0] - 8
    value = total[:step]
    square = jnp.sum(jnp.sum(value * value, axis=0, keepdims=True), axis=1, keepdims=True)
    square = jnp.broadcast_to(square, (1, lanes))
    tail = total[step : step + 1] + total[step + 1 : step + 2]
    tile = [value, *high_low(tail), *high_low(square), jnp.zeros((4, lanes), f32)]
    tile = jnp.concatenate(tile, axis=0).astype(bf16)
    out[...] = jnp.broadcast_to(tile[None], out.shape)


def places(sizes):
    nzh, nzl, nx = sizes
    return [
        ((zh * nzl + zl) * nx, pl.ds((zl * nzh + zh) * lanes, lanes))
        for zh in range(nzh)
        for zl in range(nzl)
    ]


def owned(parts, first, owner, count):
    values = [parts[first + owner * count + i].astype(f32) for i in range(count)]
    return jnp.concatenate([v[: v.shape[0] - 8] for v in values], axis=0)


def sums_of(parts, first, nx):
    planes = []
    for x in range(nx):
        value = parts[first + x].astype(f32)
        at = value.shape[0] - 8
        planes.append(value[at : at + 1] + value[at + 1 : at + 2])
    return planes[0] + planes[1], planes[2] + planes[3]


def split_kernel(sizes, parts, weight_squares, theirs, squares):
    nx = sizes[2]
    other = 1 - lax.axis_index("c")
    part = theirs.shape[0] - 8
    for first, cols in places(sizes):
        theirs[:part, cols] = owned(parts, first, other, nx // 2)
        shift, gain = sums_of(parts, first, nx)
        theirs[part:, cols] = jnp.concatenate([shift, gain, jnp.zeros((6, lanes), f32)], axis=0)
    total = jnp.sum(parts[...].astype(f32), axis=0)
    at = total.shape[0] - 6
    square = total[at : at + 1] + total[at + 1 : at + 2]
    weight_square = jnp.sum(weight_squares[...], axis=0, keepdims=True)
    weight_square = jnp.sum(weight_square, axis=1, keepdims=True)
    weight_square = jnp.broadcast_to(weight_square, (1, lanes))
    tile = jnp.concatenate([square, weight_square, jnp.zeros((6, lanes), f32)], axis=0)
    squares[...] = jnp.broadcast_to(tile[None], squares.shape)


def step_kernel(sizes, parts, arrived, squares, weight, velocity, out, gain, shift):
    nx = sizes[2]
    core = lax.axis_index("c")
    part, cout = out.shape
    half = cout // 2
    total = jnp.sum(squares[...], axis=0)
    grad_norm = jnp.sqrt(total[:1, :1])
    weight_norm = jnp.sqrt(total[1:2, :1] / (squares.shape[0] // 2))
    ratio = weight_norm / (grad_norm + weight_decay * weight_norm)

    def update(cols, weight_grad):
        decayed = weight_grad + weight_decay * weight[:, cols].astype(f32)
        out[:, cols] = momentum * velocity[:, cols] + ratio * decayed

    for first, cols in places(sizes):
        here = pl.ds(pl.multiple_of(core * half + cols.start, lanes), lanes)
        there = pl.ds(pl.multiple_of((1 - core) * half + cols.start, lanes), lanes)
        update(here, owned(parts, first, core, nx // 2))
        update(there, arrived[:part, cols])
        shift[:, here], gain[:, here] = sums_of(parts, first, nx)
        last = arrived[part:, cols]
        shift[:, there], gain[:, there] = last[:1], last[1:2]


def shape(dims, dtype):
    return jax.ShapeDtypeStruct(dims, dtype)


def whole(dims):
    return pl.BlockSpec(dims, lambda j: (0,) * len(dims))


def params(mib=24):
    return pltpu.CompilerParams(vmem_limit_bytes=mib << 20)


def call(kernel, name, operands, outs, scratch=()):
    return pl.pallas_call(
        kernel,
        grid=(1,),
        in_specs=[whole(value.shape) for value in operands],
        out_specs=[whole(out.shape) for out in outs],
        out_shape=outs,
        scratch_shapes=scratch,
        compiler_params=params(),
        name=name,
    )(*operands)


def local(block_input, activations, conv_weight, bn_gain, bn_shift, out_grad, velocity):
    rows, cin = activations.shape
    part, cout = conv_weight.shape
    half = cout // 2
    nzh, nzl, nx = sizes = tuple(lax.axis_size(a) for a in rep)
    nyh, nyl = (lax.axis_size(a) for a in y_axes)
    ny = nyh * nyl
    members = 2 * ny
    first_core = lax.axis_index("c") == 0
    gain, shift = bn_gain.reshape(1, cout), bn_shift.reshape(1, cout)

    def other_half(value):
        return jnp.where(first_core, value[:, half:], value[:, :half])

    pieces = conv_weight.reshape(part, 2, half).transpose(1, 0, 2)
    pieces = jnp.broadcast_to(pieces[None], (ny, 2, part, half)).reshape(members, part, half)
    weight = exchange(pieces, bn).reshape(cin, half)
    acts_other = swap(activations)
    block_other = swap(other_half(block_input))
    out_other = swap(other_half(out_grad))
    weight, acts_other, block_other, out_other = lax.optimization_barrier(
        (weight, acts_other, block_other, out_other)
    )

    wide = shape((rows, half), f32)
    narrow = shape((rows, half), bf16)
    sums = shape((ny, 2 * half // lanes, lanes), f32)
    conv, conv_other, moments = call(
        moments_kernel, "moments", (activations, acts_other, weight), [wide, wide, sums]
    )
    moments = exchange(moments, y_axes)
    grad, grad_other, stats = call(
        stats_kernel,
        "stats",
        (conv, conv_other, moments, gain, shift, block_input, block_other, out_grad, out_other),
        [narrow, narrow, sums],
    )
    stats = exchange(stats, y_axes)
    count = nzl * nx * nyl
    step = 2 * part // nx
    length = groups * nyh * step
    grad_conv, grad_conv_other, partial = call(
        functools.partial(weight_kernel, (nx, nyl, nyh)),
        "weight_partial",
        (conv, conv_other, moments, stats, gain, grad, grad_other, activations, acts_other),
        [narrow, narrow, shape((count, length + 16, lanes), bf16)],
        [pltpu.VMEM((cin, chunk), f32)] + [pltpu.VMEM((cin, rows), bf16)] * 2,
    )
    act, act_other, weight_squares = call(
        act_kernel,
        "act_grad",
        (grad_conv, grad_conv_other, weight),
        [shape((rows, cin), f32), shape((rows, cin), bf16), shape((8, lanes), f32)],
    )
    partial, act_other = lax.optimization_barrier((partial, act_other))
    act_grad = (act + swap(act_other).astype(f32)).astype(bf16)

    (partial,) = call(
        functools.partial(near_kernel, nyh),
        "near_sum",
        (exchange(partial, near),),
        [shape((nzh * nyh, step + 8, lanes), bf16)],
        [pltpu.VMEM((length + 16, lanes), f32)],
    )
    (ready,) = call(
        far_kernel,
        "far_sum",
        (exchange(partial, far),),
        [shape((nzh * nzl * nx, step + 8, lanes), bf16)],
    )
    ready = exchange(ready, rep)
    theirs, squares = call(
        functools.partial(split_kernel, sizes),
        "split",
        (ready, weight_squares),
        [shape((part + 8, half), f32), shape((members, 8, lanes), f32)],
    )
    arrived = swap(theirs)
    squares = exchange(squares, bn)
    new_velocity, gain_grad, shift_grad = call(
        functools.partial(step_kernel, sizes),
        "step",
        (ready, arrived, squares, conv_weight, velocity),
        [shape((part, cout), f32), shape((1, cout), f32), shape((1, cout), f32)],
    )
    return (act_grad, gain_grad.reshape(cout), shift_grad.reshape(cout), new_velocity)


def solution(mesh, dims=(4, 2, 4, 4, 2, 2)):
    fine = Mesh(mesh.devices.reshape(dims), rep + bn)
    every = P(rep + bn, None)
    return jax.shard_map(
        local,
        mesh=fine,
        in_specs=(every, every, P(bn, None), P(), P(), every, P(bn, None)),
        out_specs=(every, P(), P(), P(bn, None)),
        check_vma=False,
    )
```

```python
import functools

import jax
import jax.numpy as jnp
from jax import lax
from jax.experimental import pallas as pl
from jax.experimental.pallas import tpu as pltpu
from jax.sharding import Mesh, PartitionSpec as P

epsilon = 1e-05
weight_decay = 5e-05
momentum = 0.9
f32, bf16 = jnp.float32, jnp.bfloat16
rep = ("zh", "zl", "x")
y_axes = ("yh", "yl")
bn = ("yh", "yl", "c")
near = ("zl", "x", "yl")
far = ("zh", "yh")
lanes = 128
chunk = 512
groups = chunk // lanes


def swap(value):
    return lax.ppermute(value, "c", [(0, 1), (1, 0)])


def exchange(pieces, axis):
    return lax.all_to_all(pieces, axis, 0, 0, tiled=True)


def copies(value, axis):
    n = lax.axis_size(axis)
    return exchange(jnp.broadcast_to(value[None], (n, *value.shape)), axis)


def fold(row):
    return [row[:, q * lanes : (q + 1) * lanes] for q in range(groups)]


def unfold(tile):
    return jnp.concatenate([tile[q : q + 1] for q in range(groups)], axis=1)


def high_low(value):
    high = value.astype(bf16).astype(f32)
    return high, value - high


def columns(width):
    return [pl.ds(start, chunk) for start in range(0, width, chunk)]


def moments_kernel(acts, acts_other, weight, conv, conv_other, moments):
    count = 2 * conv.shape[0]
    for j, cols in enumerate(columns(conv.shape[1])):
        both = []
        for rows, out in ((acts, conv), (acts_other, conv_other)):
            value = jnp.dot(rows[...], weight[:, cols], preferred_element_type=f32)
            out[:, cols] = value
            both.append(value)
        mean = sum(jnp.sum(value, axis=0, keepdims=True) for value in both) / count
        square = sum(jnp.sum((v - mean) * (v - mean), axis=0, keepdims=True) for v in both)
        tile = jnp.concatenate(fold(mean) + fold(square), axis=0)
        moments[:, 8 * j : 8 * j + 8] = jnp.broadcast_to(tile[None], (moments.shape[0], 8, lanes))


def pooled(moments, rows):
    members = moments.shape[0]
    means, squares = moments[:, :groups], moments[:, groups:]
    mean = jnp.sum(means, axis=0) / members
    offset = means - mean[None]
    square = jnp.sum(squares, axis=0) + rows * jnp.sum(offset * offset, axis=0)
    inv_std = lax.rsqrt(square / (rows * members) + epsilon)
    return unfold(mean), unfold(inv_std)


def stats_kernel(
    conv, conv_other, moments, gain, shift, block, block_other, out, out_other, grad, grad_other, stats
):
    rows, half = conv.shape
    core = lax.axis_index("c")
    for j, cols in enumerate(columns(half)):
        place = pl.ds(pl.multiple_of(core * half + j * chunk, chunk), chunk)
        mean, inv_std = pooled(moments[:, 8 * j : 8 * j + 8], 2 * rows)
        scale, bias = gain[:, place] * inv_std, shift[:, place]
        sum_grad = sum_cross = 0.0
        for of, added, incoming, result in (
            (conv, block[:, place], out[:, place], grad),
            (conv_other, block_other[:, cols], out_other[:, cols], grad_other),
        ):
            centered = of[:, cols] - mean
            summed = centered * scale + bias + added.astype(f32)
            value = jnp.where(summed > 0.0, incoming.astype(f32), 0.0)
            result[:, cols] = value.astype(bf16)
            sum_grad += jnp.sum(value, axis=0, keepdims=True)
            sum_cross += jnp.sum(value * centered, axis=0, keepdims=True)
        tile = jnp.concatenate(fold(sum_grad) + fold(sum_cross * inv_std), axis=0)
        stats[:, 8 * j : 8 * j + 8] = jnp.broadcast_to(tile[None], (stats.shape[0], 8, lanes))


def weight_kernel(
    sizes,
    conv,
    conv_other,
    moments,
    stats,
    gain,
    grad,
    grad_other,
    acts,
    acts_other,
    grad_conv,
    grad_conv_other,
    out,
    wide,
    acts_t,
    acts_t_other,
):
    nx, nyl, nyh = sizes
    core = lax.axis_index("c")
    rows, half = conv.shape
    group_rows = 2 * rows * moments.shape[0]
    part = wide.shape[0] // (nyl * nyh)
    step = part // nx
    length = groups * nyh * step
    acts_t[...] = acts[...].T
    acts_t_other[...] = acts_other[...].T
    for j, cols in enumerate(columns(half)):
        place = pl.ds(pl.multiple_of(core * half + j * chunk, chunk), chunk)
        mean, inv_std = pooled(moments[:, 8 * j : 8 * j + 8], 2 * rows)
        sums = jnp.sum(stats[:, 8 * j : 8 * j + 8], axis=0)
        sum_grad, sum_cross = sums[:groups], sums[groups:]
        shift = unfold(sum_grad) / group_rows
        slope = inv_std * unfold(sum_cross) / group_rows
        scale = gain[:, place] * inv_std
        product = 0.0
        for of, pre, left, result in (
            (conv, grad, acts_t, grad_conv),
            (conv_other, grad_other, acts_t_other, grad_conv_other),
        ):
            value = pre[:, cols].astype(f32) - shift - (of[:, cols] - mean) * slope
            narrow = (scale * value).astype(bf16)
            result[:, cols] = narrow
            product += jnp.dot(left[...], narrow, preferred_element_type=f32)
        wide[...] = product
        planes = (*high_low(sum_grad), *high_low(sum_cross))
        for x in range(nx):
            last = jnp.concatenate(
                [planes[x] / (nyl * nyh), jnp.zeros((16 - groups, lanes), f32)], axis=0
            )
            for yl in range(nyl):
                piece = (j * nx + x) * nyl + yl
                rows_of = [
                    wide[
                        pl.ds((yh * nyl + yl) * part + step * x, step), pl.ds(q * lanes, lanes)
                    ]
                    for q in range(groups)
                    for yh in range(nyh)
                ]
                out[piece, :length] = jnp.concatenate(rows_of, axis=0).astype(bf16)
                out[piece, length:] = last.astype(bf16)


def act_kernel(grad_conv, grad_conv_other, weight, act, act_other, squares):
    dims = (((1,), (1,)), ((), ()))
    act[...] = lax.dot_general(grad_conv[...], weight[...], dims, preferred_element_type=f32)
    act_other[...] = lax.dot_general(
        grad_conv_other[...], weight[...], dims, preferred_element_type=f32
    ).astype(bf16)
    total = jnp.zeros((8, lanes), f32)
    for cols in columns(weight.shape[1]):
        wide = weight[:, cols].astype(f32)
        total += sum(fold(jnp.sum((wide * wide).reshape(-1, 8, chunk), axis=0)))
    squares[...] = total


def near_kernel(nyh, received, out, total):
    count, depth, _ = out.shape
    step = depth - 8
    total[...] = jnp.sum(received[...].astype(f32), axis=0)
    for zh in range(count // nyh):
        base = count * step + zh
        high, low = high_low(total[base : base + 1, :])
        extra = jnp.concatenate([high, low, jnp.zeros((6, lanes), f32)], axis=0)
        for yh in range(nyh):
            at = (zh * nyh + yh) * step
            tile = jnp.concatenate([total[at : at + step, :], extra], axis=0)
            out[zh * nyh + yh] = tile.astype(bf16)


def far_kernel(received, out):
    total = jnp.sum(received[...].astype(f32), axis=0)
    step = total.shape[0] - 8
    value = total[:step]
    square = jnp.sum(jnp.sum(value * value, axis=0, keepdims=True), axis=1, keepdims=True)
    square = jnp.broadcast_to(square, (1, lanes))
    tail = total[step : step + 1] + total[step + 1 : step + 2]
    tile = [value, *high_low(tail), *high_low(square), jnp.zeros((4, lanes), f32)]
    tile = jnp.concatenate(tile, axis=0).astype(bf16)
    out[...] = jnp.broadcast_to(tile[None], out.shape)


def places(sizes):
    nzh, nzl, nx = sizes
    return [
        ((zh * nzl + zl) * nx, pl.ds((zl * nzh + zh) * lanes, lanes))
        for zh in range(nzh)
        for zl in range(nzl)
    ]


def owned(parts, first, owner, count):
    values = [parts[first + owner * count + i].astype(f32) for i in range(count)]
    return jnp.concatenate([v[: v.shape[0] - 8] for v in values], axis=0)


def sums_of(parts, first, nx):
    planes = []
    for x in range(nx):
        value = parts[first + x].astype(f32)
        at = value.shape[0] - 8
        planes.append(value[at : at + 1] + value[at + 1 : at + 2])
    return planes[0] + planes[1], planes[2] + planes[3]


def split_kernel(sizes, parts, weight_squares, theirs, squares):
    nx = sizes[2]
    other = 1 - lax.axis_index("c")
    part = theirs.shape[0] - 8
    for first, cols in places(sizes):
        theirs[:part, cols] = owned(parts, first, other, nx // 2)
        shift, gain = sums_of(parts, first, nx)
        theirs[part:, cols] = jnp.concatenate([shift, gain, jnp.zeros((6, lanes), f32)], axis=0)
    total = jnp.sum(parts[...].astype(f32), axis=0)
    at = total.shape[0] - 6
    square = total[at : at + 1] + total[at + 1 : at + 2]
    weight_square = jnp.sum(weight_squares[...], axis=0, keepdims=True)
    weight_square = jnp.sum(weight_square, axis=1, keepdims=True)
    weight_square = jnp.broadcast_to(weight_square, (1, lanes))
    tile = jnp.concatenate([square, weight_square, jnp.zeros((6, lanes), f32)], axis=0)
    squares[...] = jnp.broadcast_to(tile[None], squares.shape)


def step_kernel(sizes, parts, arrived, squares, weight, velocity, out, gain, shift):
    nx = sizes[2]
    core = lax.axis_index("c")
    part, cout = out.shape
    half = cout // 2
    total = jnp.sum(squares[...], axis=0)
    grad_norm = jnp.sqrt(total[:1, :1])
    weight_norm = jnp.sqrt(total[1:2, :1] / (squares.shape[0] // 2))
    ratio = weight_norm / (grad_norm + weight_decay * weight_norm)

    def update(cols, weight_grad):
        decayed = weight_grad + weight_decay * weight[:, cols].astype(f32)
        out[:, cols] = momentum * velocity[:, cols] + ratio * decayed

    for first, cols in places(sizes):
        here = pl.ds(pl.multiple_of(core * half + cols.start, lanes), lanes)
        there = pl.ds(pl.multiple_of((1 - core) * half + cols.start, lanes), lanes)
        update(here, owned(parts, first, core, nx // 2))
        update(there, arrived[:part, cols])
        shift[:, here], gain[:, here] = sums_of(parts, first, nx)
        last = arrived[part:, cols]
        shift[:, there], gain[:, there] = last[:1], last[1:2]


def shape(dims, dtype):
    return jax.ShapeDtypeStruct(dims, dtype)


def whole(dims):
    return pl.BlockSpec(dims, lambda j: (0,) * len(dims))


def params(mib=24):
    return pltpu.CompilerParams(vmem_limit_bytes=mib << 20)


def call(kernel, name, operands, outs, scratch=()):
    return pl.pallas_call(
        kernel,
        grid=(1,),
        in_specs=[whole(value.shape) for value in operands],
        out_specs=[whole(out.shape) for out in outs],
        out_shape=outs,
        scratch_shapes=scratch,
        compiler_params=params(),
        name=name,
    )(*operands)


def local(block_input, activations, conv_weight, bn_gain, bn_shift, out_grad, velocity):
    rows, cin = activations.shape
    part, cout = conv_weight.shape
    half = cout // 2
    nzh, nzl, nx = sizes = tuple(lax.axis_size(a) for a in rep)
    nyh, nyl = (lax.axis_size(a) for a in y_axes)
    ny = nyh * nyl
    members = 2 * ny
    first_core = lax.axis_index("c") == 0
    gain, shift = bn_gain.reshape(1, cout), bn_shift.reshape(1, cout)

    def other_half(value):
        return jnp.where(first_core, value[:, half:], value[:, :half])

    pieces = jnp.stack([conv_weight[:, :half], conv_weight[:, half:]])
    pieces = jnp.broadcast_to(pieces[None], (ny, 2, part, half)).reshape(members, part, half)
    weight = exchange(pieces, bn).reshape(cin, half)
    acts_other = swap(activations)
    block_other = swap(other_half(block_input))
    out_other = swap(other_half(out_grad))
    weight, acts_other = lax.optimization_barrier((weight, acts_other))

    wide = shape((rows, half), f32)
    narrow = shape((rows, half), bf16)
    sums = shape((ny, 2 * half // lanes, lanes), f32)
    conv, conv_other, moments = call(
        moments_kernel, "moments", (activations, acts_other, weight), [wide, wide, sums]
    )
    moments, block_other, out_other = lax.optimization_barrier((moments, block_other, out_other))
    moments = exchange(moments, y_axes)
    grad, grad_other, stats = call(
        stats_kernel,
        "stats",
        (conv, conv_other, moments, gain, shift, block_input, block_other, out_grad, out_other),
        [narrow, narrow, sums],
    )
    stats = exchange(stats, y_axes)
    count = nzl * nx * nyl
    step = 2 * part // nx
    length = groups * nyh * step
    grad_conv, grad_conv_other, partial = call(
        functools.partial(weight_kernel, (nx, nyl, nyh)),
        "weight_partial",
        (conv, conv_other, moments, stats, gain, grad, grad_other, activations, acts_other),
        [narrow, narrow, shape((count, length + 16, lanes), bf16)],
        [pltpu.VMEM((cin, chunk), f32)] + [pltpu.VMEM((cin, rows), bf16)] * 2,
    )
    act, act_other, weight_squares = call(
        act_kernel,
        "act_grad",
        (grad_conv, grad_conv_other, weight),
        [shape((rows, cin), f32), shape((rows, cin), bf16), shape((8, lanes), f32)],
    )
    partial, act_other = lax.optimization_barrier((partial, act_other))
    act_grad = (act + swap(act_other).astype(f32)).astype(bf16)
    partial, act_grad = lax.optimization_barrier((exchange(partial, near), act_grad))

    (partial,) = call(
        functools.partial(near_kernel, nyh),
        "near_sum",
        (partial,),
        [shape((nzh * nyh, step + 8, lanes), bf16)],
        [pltpu.VMEM((length + 16, lanes), f32)],
    )
    (ready,) = call(
        far_kernel,
        "far_sum",
        (exchange(partial, far),),
        [shape((nzh * nzl * nx, step + 8, lanes), bf16)],
    )
    ready = exchange(ready, rep)
    theirs, squares = call(
        functools.partial(split_kernel, sizes),
        "split",
        (ready, weight_squares),
        [shape((part + 8, half), f32), shape((members, 8, lanes), f32)],
    )
    arrived = swap(theirs)
    squares = exchange(squares, bn)
    new_velocity, gain_grad, shift_grad = call(
        functools.partial(step_kernel, sizes),
        "step",
        (ready, arrived, squares, conv_weight, velocity),
        [shape((part, cout), f32), shape((1, cout), f32), shape((1, cout), f32)],
    )
    return (act_grad, gain_grad.reshape(cout), shift_grad.reshape(cout), new_velocity)


def solution(mesh, dims=(4, 2, 4, 4, 2, 2)):
    fine = Mesh(mesh.devices.reshape(dims), rep + bn)
    every = P(rep + bn, None)
    return jax.shard_map(
        local,
        mesh=fine,
        in_specs=(every, every, P(bn, None), P(), P(), every, P(bn, None)),
        out_specs=(every, P(), P(), P(bn, None)),
        check_vma=False,
    )
```

```python
import functools

import jax
import jax.numpy as jnp
from jax import lax
from jax.experimental import pallas as pl
from jax.experimental.pallas import tpu as pltpu
from jax.sharding import Mesh, PartitionSpec as P

epsilon = 1e-05
weight_decay = 5e-05
momentum = 0.9
f32, bf16 = jnp.float32, jnp.bfloat16
rep = ("zh", "zl", "x")
y_axes = ("yh", "yl")
bn = ("yh", "yl", "c")
near = ("zl", "x", "yl")
far = ("zh", "yh")
lanes = 128
chunk = 512
groups = chunk // lanes


def swap(value):
    return lax.ppermute(value, "c", [(0, 1), (1, 0)])


def exchange(pieces, axis):
    return lax.all_to_all(pieces, axis, 0, 0, tiled=True)


def copies(value, axis):
    n = lax.axis_size(axis)
    return exchange(jnp.broadcast_to(value[None], (n, *value.shape)), axis)


def fold(row):
    return [row[:, q * lanes : (q + 1) * lanes] for q in range(groups)]


def unfold(tile):
    return jnp.concatenate([tile[q : q + 1] for q in range(groups)], axis=1)


def high_low(value):
    high = value.astype(bf16).astype(f32)
    return high, value - high


def columns(width):
    return [pl.ds(start, chunk) for start in range(0, width, chunk)]


def pieces_kernel(weight, out, sems):
    half = out.shape[2]
    copies_out = [
        pltpu.make_async_copy(
            weight.at[:, pl.ds(i % 2 * half, half)], out.at[i], sems.at[i]
        )
        for i in range(out.shape[0])
    ]
    for copy in copies_out:
        copy.start()
    for copy in copies_out:
        copy.wait()


def moments_kernel(acts, acts_other, weight, conv, conv_other, moments):
    count = 2 * conv.shape[0]
    for j, cols in enumerate(columns(conv.shape[1])):
        both = []
        for rows, out in ((acts, conv), (acts_other, conv_other)):
            value = jnp.dot(rows[...], weight[:, cols], preferred_element_type=f32)
            out[:, cols] = value
            both.append(value)
        mean = sum(jnp.sum(value, axis=0, keepdims=True) for value in both) / count
        square = sum(jnp.sum((v - mean) * (v - mean), axis=0, keepdims=True) for v in both)
        tile = jnp.concatenate(fold(mean) + fold(square), axis=0)
        moments[:, 8 * j : 8 * j + 8] = jnp.broadcast_to(tile[None], (moments.shape[0], 8, lanes))


def pooled(moments, rows):
    members = moments.shape[0]
    means, squares = moments[:, :groups], moments[:, groups:]
    mean = jnp.sum(means, axis=0) / members
    offset = means - mean[None]
    square = jnp.sum(squares, axis=0) + rows * jnp.sum(offset * offset, axis=0)
    inv_std = lax.rsqrt(square / (rows * members) + epsilon)
    return unfold(mean), unfold(inv_std)


def stats_kernel(
    conv,
    conv_other,
    moments,
    gain,
    shift,
    block,
    out,
    block_far,
    out_far,
    grad,
    grad_other,
    stats,
    block_other,
    out_other,
    sems,
):
    rows, half = conv.shape
    core = lax.axis_index("c")
    loads = [
        pltpu.make_async_copy(block_far, block_other, sems.at[0]),
        pltpu.make_async_copy(out_far, out_other, sems.at[1]),
    ]
    for load in loads:
        load.start()
    scales = []
    for j, cols in enumerate(columns(half)):
        place = pl.ds(pl.multiple_of(core * half + j * chunk, chunk), chunk)
        mean, inv_std = pooled(moments[:, 8 * j : 8 * j + 8], 2 * rows)
        scales.append((cols, place, mean, inv_std, gain[:, place] * inv_std, shift[:, place]))

    def sums(of, added, incoming, result, cols, mean, scale, bias):
        centered = of[:, cols] - mean
        summed = centered * scale + bias + added.astype(f32)
        value = jnp.where(summed > 0.0, incoming.astype(f32), 0.0)
        result[:, cols] = value.astype(bf16)
        return (
            jnp.sum(value, axis=0, keepdims=True),
            jnp.sum(value * centered, axis=0, keepdims=True),
        )

    near_sums = [
        sums(conv, block[:, place], out[:, place], grad, cols, mean, scale, bias)
        for cols, place, mean, _, scale, bias in scales
    ]
    for load in loads:
        load.wait()
    for j, (cols, _, mean, inv_std, scale, bias) in enumerate(scales):
        sum_grad, sum_cross = sums(
            conv_other, block_other[:, cols], out_other[:, cols], grad_other, cols, mean, scale, bias
        )
        sum_grad += near_sums[j][0]
        sum_cross += near_sums[j][1]
        tile = jnp.concatenate(fold(sum_grad) + fold(sum_cross * inv_std), axis=0)
        stats[:, 8 * j : 8 * j + 8] = jnp.broadcast_to(tile[None], (stats.shape[0], 8, lanes))


def weight_kernel(
    sizes,
    conv,
    conv_other,
    moments,
    stats,
    gain,
    grad,
    grad_other,
    acts,
    acts_other,
    weight,
    act,
    act_other,
    squares,
    result_out,
    wide,
    acts_t,
    acts_t_other,
    grad_conv,
    grad_conv_other,
    out,
    sems,
):
    nx, nyl, nyh = sizes
    core = lax.axis_index("c")
    rows, half = conv.shape
    group_rows = 2 * rows * moments.shape[0]
    part = wide.shape[0] // (nyl * nyh)
    step = part // nx
    length = groups * nyh * step
    acts_t[...] = acts[...].T
    acts_t_other[...] = acts_other[...].T
    writes = []
    for j, cols in enumerate(columns(half)):
        place = pl.ds(pl.multiple_of(core * half + j * chunk, chunk), chunk)
        mean, inv_std = pooled(moments[:, 8 * j : 8 * j + 8], 2 * rows)
        sums = jnp.sum(stats[:, 8 * j : 8 * j + 8], axis=0)
        sum_grad, sum_cross = sums[:groups], sums[groups:]
        shift = unfold(sum_grad) / group_rows
        slope = inv_std * unfold(sum_cross) / group_rows
        scale = gain[:, place] * inv_std
        product = 0.0
        for of, pre, left, result in (
            (conv, grad, acts_t, grad_conv),
            (conv_other, grad_other, acts_t_other, grad_conv_other),
        ):
            value = pre[:, cols].astype(f32) - shift - (of[:, cols] - mean) * slope
            narrow = (scale * value).astype(bf16)
            result[:, cols] = narrow
            product += jnp.dot(left[...], narrow, preferred_element_type=f32)
        wide[...] = product
        planes = (*high_low(sum_grad), *high_low(sum_cross))
        for x in range(nx):
            last = jnp.concatenate(
                [planes[x] / (nyl * nyh), jnp.zeros((16 - groups, lanes), f32)], axis=0
            )
            for yl in range(nyl):
                piece = (j * nx + x) * nyl + yl
                rows_of = [
                    wide[
                        pl.ds((yh * nyl + yl) * part + step * x, step), pl.ds(q * lanes, lanes)
                    ]
                    for q in range(groups)
                    for yh in range(nyh)
                ]
                out[piece, :length] = jnp.concatenate(rows_of, axis=0).astype(bf16)
                out[piece, length:] = last.astype(bf16)
        ready = pl.ds(j * nx * nyl, nx * nyl)
        writes.append(pltpu.make_async_copy(out.at[ready], result_out.at[ready], sems.at[j]))
        writes[-1].start()

    dims = (((1,), (1,)), ((), ()))
    act[...] = lax.dot_general(grad_conv[...], weight[...], dims, preferred_element_type=f32)
    act_other[...] = lax.dot_general(
        grad_conv_other[...], weight[...], dims, preferred_element_type=f32
    ).astype(bf16)
    total = jnp.zeros((8, lanes), f32)
    for cols in columns(weight.shape[1]):
        value = weight[:, cols].astype(f32)
        total += sum(fold(jnp.sum((value * value).reshape(-1, 8, chunk), axis=0)))
    squares[...] = total
    for write in writes:
        write.wait()


def near_kernel(nyh, received, out, total):
    count, depth, _ = out.shape
    step = depth - 8
    total[...] = jnp.sum(received[...].astype(f32), axis=0)
    for zh in range(count // nyh):
        base = count * step + zh
        high, low = high_low(total[base : base + 1, :])
        extra = jnp.concatenate([high, low, jnp.zeros((6, lanes), f32)], axis=0)
        for yh in range(nyh):
            at = (zh * nyh + yh) * step
            tile = jnp.concatenate([total[at : at + step, :], extra], axis=0)
            out[zh * nyh + yh] = tile.astype(bf16)


def far_kernel(received, out):
    total = jnp.sum(received[...].astype(f32), axis=0)
    step = total.shape[0] - 8
    value = total[:step]
    square = jnp.sum(jnp.sum(value * value, axis=0, keepdims=True), axis=1, keepdims=True)
    square = jnp.broadcast_to(square, (1, lanes))
    tail = total[step : step + 1] + total[step + 1 : step + 2]
    tile = [value, *high_low(tail), *high_low(square), jnp.zeros((4, lanes), f32)]
    tile = jnp.concatenate(tile, axis=0).astype(bf16)
    out[...] = jnp.broadcast_to(tile[None], out.shape)


def places(sizes):
    nzh, nzl, nx = sizes
    return [
        ((zh * nzl + zl) * nx, pl.ds((zl * nzh + zh) * lanes, lanes))
        for zh in range(nzh)
        for zl in range(nzl)
    ]


def owned(parts, first, owner, count):
    values = [parts[first + owner * count + i].astype(f32) for i in range(count)]
    return jnp.concatenate([v[: v.shape[0] - 8] for v in values], axis=0)


def sums_of(parts, first, nx):
    planes = []
    for x in range(nx):
        value = parts[first + x].astype(f32)
        at = value.shape[0] - 8
        planes.append(value[at : at + 1] + value[at + 1 : at + 2])
    return planes[0] + planes[1], planes[2] + planes[3]


def split_kernel(sizes, parts, weight_squares, theirs, squares):
    nx = sizes[2]
    other = 1 - lax.axis_index("c")
    part = theirs.shape[0] - 8
    for first, cols in places(sizes):
        theirs[:part, cols] = owned(parts, first, other, nx // 2)
        shift, gain = sums_of(parts, first, nx)
        theirs[part:, cols] = jnp.concatenate([shift, gain, jnp.zeros((6, lanes), f32)], axis=0)
    total = jnp.sum(parts[...].astype(f32), axis=0)
    at = total.shape[0] - 6
    square = total[at : at + 1] + total[at + 1 : at + 2]
    weight_square = jnp.sum(weight_squares[...], axis=0, keepdims=True)
    weight_square = jnp.sum(weight_square, axis=1, keepdims=True)
    weight_square = jnp.broadcast_to(weight_square, (1, lanes))
    tile = jnp.concatenate([square, weight_square, jnp.zeros((6, lanes), f32)], axis=0)
    squares[...] = jnp.broadcast_to(tile[None], squares.shape)


def step_kernel(sizes, parts, arrived, squares, weight, velocity, out, gain, shift):
    nx = sizes[2]
    core = lax.axis_index("c")
    part, cout = out.shape
    half = cout // 2
    total = jnp.sum(squares[...], axis=0)
    grad_norm = jnp.sqrt(total[:1, :1])
    weight_norm = jnp.sqrt(total[1:2, :1] / (squares.shape[0] // 2))
    ratio = weight_norm / (grad_norm + weight_decay * weight_norm)

    def update(cols, weight_grad):
        decayed = weight_grad + weight_decay * weight[:, cols].astype(f32)
        out[:, cols] = momentum * velocity[:, cols] + ratio * decayed

    for first, cols in places(sizes):
        here = pl.ds(pl.multiple_of(core * half + cols.start, lanes), lanes)
        there = pl.ds(pl.multiple_of((1 - core) * half + cols.start, lanes), lanes)
        update(here, owned(parts, first, core, nx // 2))
        update(there, arrived[:part, cols])
        shift[:, here], gain[:, here] = sums_of(parts, first, nx)
        last = arrived[part:, cols]
        shift[:, there], gain[:, there] = last[:1], last[1:2]


def shape(dims, dtype):
    return jax.ShapeDtypeStruct(dims, dtype)


def whole(dims):
    return pl.BlockSpec(dims, lambda j: (0,) * len(dims))


def params(mib=24):
    return pltpu.CompilerParams(vmem_limit_bytes=mib << 20)


def call(kernel, name, operands, outs, scratch=(), loaded=0, written=None):
    anywhere = pl.BlockSpec(memory_space=pl.ANY)
    at = len(operands) - loaded
    in_specs = [whole(value.shape) for value in operands[:at]] + [anywhere] * loaded
    out_specs = [whole(out.shape) for out in outs]
    if written is not None:
        out_specs.append(anywhere)
        outs = [*outs, pltpu.HBM(written.shape, written.dtype)]
    return pl.pallas_call(
        kernel,
        grid=(1,),
        in_specs=in_specs,
        out_specs=out_specs,
        out_shape=outs,
        scratch_shapes=scratch,
        compiler_params=params(),
        name=name,
    )(*operands)


def local(block_input, activations, conv_weight, bn_gain, bn_shift, out_grad, velocity):
    rows, cin = activations.shape
    part, cout = conv_weight.shape
    half = cout // 2
    nzh, nzl, nx = sizes = tuple(lax.axis_size(a) for a in rep)
    nyh, nyl = (lax.axis_size(a) for a in y_axes)
    ny = nyh * nyl
    members = 2 * ny
    first_core = lax.axis_index("c") == 0
    gain, shift = bn_gain.reshape(1, cout), bn_shift.reshape(1, cout)

    def other_half(value):
        return jnp.where(first_core, value[:, half:], value[:, :half])

    (pieces,) = call(
        pieces_kernel,
        "pieces",
        (conv_weight,),
        [],
        [pltpu.SemaphoreType.DMA((members,))],
        written=shape((members, part, half), bf16),
    )
    weight = exchange(pieces, bn).reshape(cin, half)
    acts_other = swap(activations)
    block_other = swap(other_half(block_input))
    out_other = swap(other_half(out_grad))
    weight, acts_other = lax.optimization_barrier((weight, acts_other))

    wide = shape((rows, half), f32)
    narrow = shape((rows, half), bf16)
    sums = shape((ny, 2 * half // lanes, lanes), f32)
    conv, conv_other, moments = call(
        moments_kernel, "moments", (activations, acts_other, weight), [wide, wide, sums]
    )
    moments, block_other, out_other = lax.optimization_barrier((moments, block_other, out_other))
    moments = exchange(moments, y_axes)
    grad, grad_other, stats = call(
        stats_kernel,
        "stats",
        (conv, conv_other, moments, gain, shift, block_input, out_grad, block_other, out_other),
        [narrow, narrow, sums],
        [pltpu.VMEM((rows, half), bf16)] * 2 + [pltpu.SemaphoreType.DMA((2,))],
        loaded=2,
    )
    stats = exchange(stats, y_axes)
    count = nzl * nx * nyl
    step = 2 * part // nx
    length = groups * nyh * step
    act, act_other, weight_squares, partial = call(
        functools.partial(weight_kernel, (nx, nyl, nyh)),
        "weight_partial",
        (conv, conv_other, moments, stats, gain, grad, grad_other, activations, acts_other, weight),
        [shape((rows, cin), f32), shape((rows, cin), bf16), shape((8, lanes), f32)],
        [pltpu.VMEM((cin, chunk), f32)]
        + [pltpu.VMEM((cin, rows), bf16)] * 2
        + [pltpu.VMEM((rows, half), bf16)] * 2
        + [pltpu.VMEM((count, length + 16, lanes), bf16)]
        + [pltpu.SemaphoreType.DMA((half // chunk,))],
        written=shape((count, length + 16, lanes), bf16),
    )
    act_grad = (act + swap(act_other).astype(f32)).astype(bf16)
    partial, act_grad = lax.optimization_barrier((exchange(partial, near), act_grad))

    (partial,) = call(
        functools.partial(near_kernel, nyh),
        "near_sum",
        (partial,),
        [shape((nzh * nyh, step + 8, lanes), bf16)],
        [pltpu.VMEM((length + 16, lanes), f32)],
    )
    (ready,) = call(
        far_kernel,
        "far_sum",
        (exchange(partial, far),),
        [shape((nzh * nzl * nx, step + 8, lanes), bf16)],
    )
    ready = exchange(ready, rep)
    theirs, squares = call(
        functools.partial(split_kernel, sizes),
        "split",
        (ready, weight_squares),
        [shape((part + 8, half), f32), shape((members, 8, lanes), f32)],
    )
    arrived = swap(theirs)
    squares = exchange(squares, bn)
    new_velocity, gain_grad, shift_grad = call(
        functools.partial(step_kernel, sizes),
        "step",
        (ready, arrived, squares, conv_weight, velocity),
        [shape((part, cout), f32), shape((1, cout), f32), shape((1, cout), f32)],
    )
    return (act_grad, gain_grad.reshape(cout), shift_grad.reshape(cout), new_velocity)


def solution(mesh, dims=(4, 2, 4, 4, 2, 2)):
    fine = Mesh(mesh.devices.reshape(dims), rep + bn)
    every = P(rep + bn, None)
    return jax.shard_map(
        local,
        mesh=fine,
        in_specs=(every, every, P(bn, None), P(), P(), every, P(bn, None)),
        out_specs=(every, P(), P(), P(bn, None)),
        check_vma=False,
    )
```

```python
import functools

import jax
import jax.numpy as jnp
from jax import lax
from jax.experimental import pallas as pl
from jax.experimental.pallas import tpu as pltpu
from jax.sharding import Mesh, PartitionSpec as P

epsilon = 1e-05
weight_decay = 5e-05
momentum = 0.9
f32, bf16 = jnp.float32, jnp.bfloat16
rep = ("zh", "zl", "x")
y_axes = ("yh", "yl")
bn = ("yh", "yl", "c")
near = ("zl", "x", "yl")
far = ("zh", "yh")
lanes = 128
chunk = 512
groups = chunk // lanes


def swap(value):
    return lax.ppermute(value, "c", [(0, 1), (1, 0)])


def exchange(pieces, axis):
    return lax.all_to_all(pieces, axis, 0, 0, tiled=True)


def copies(value, axis):
    n = lax.axis_size(axis)
    return exchange(jnp.broadcast_to(value[None], (n, *value.shape)), axis)


def fold(row):
    return [row[:, q * lanes : (q + 1) * lanes] for q in range(groups)]


def unfold(tile):
    return jnp.concatenate([tile[q : q + 1] for q in range(groups)], axis=1)


def high_low(value):
    high = value.astype(bf16).astype(f32)
    return high, value - high


def columns(width):
    return [pl.ds(start, chunk) for start in range(0, width, chunk)]


def pieces_kernel(weight, out, sems):
    half = out.shape[2]
    copies_out = [
        pltpu.make_async_copy(
            weight.at[:, pl.ds(i % 2 * half, half)], out.at[i], sems.at[i]
        )
        for i in range(out.shape[0])
    ]
    for copy in copies_out:
        copy.start()
    for copy in copies_out:
        copy.wait()


def moments_kernel(acts, acts_other, weight, conv, conv_other, moments):
    count = 2 * conv.shape[0]
    for j, cols in enumerate(columns(conv.shape[1])):
        both = []
        for rows, out in ((acts, conv), (acts_other, conv_other)):
            value = jnp.dot(rows[...], weight[:, cols], preferred_element_type=f32)
            out[:, cols] = value
            both.append(value)
        mean = sum(jnp.sum(value, axis=0, keepdims=True) for value in both) / count
        square = sum(jnp.sum((v - mean) * (v - mean), axis=0, keepdims=True) for v in both)
        tile = jnp.concatenate(fold(mean) + fold(square), axis=0)
        moments[:, 8 * j : 8 * j + 8] = jnp.broadcast_to(tile[None], (moments.shape[0], 8, lanes))


def pooled(moments, rows):
    members = moments.shape[0]
    means, squares = moments[:, :groups], moments[:, groups:]
    mean = jnp.sum(means, axis=0) / members
    offset = means - mean[None]
    square = jnp.sum(squares, axis=0) + rows * jnp.sum(offset * offset, axis=0)
    inv_std = lax.rsqrt(square / (rows * members) + epsilon)
    return unfold(mean), unfold(inv_std)


def stats_kernel(
    conv,
    conv_other,
    moments,
    gain,
    shift,
    block,
    out,
    block_far,
    out_far,
    grad,
    grad_other,
    stats,
    block_other,
    out_other,
    sems,
):
    rows, half = conv.shape
    core = lax.axis_index("c")
    loads = [
        pltpu.make_async_copy(block_far, block_other, sems.at[0]),
        pltpu.make_async_copy(out_far, out_other, sems.at[1]),
    ]
    for load in loads:
        load.start()
    scales = []
    for j, cols in enumerate(columns(half)):
        place = pl.ds(pl.multiple_of(core * half + j * chunk, chunk), chunk)
        mean, inv_std = pooled(moments[:, 8 * j : 8 * j + 8], 2 * rows)
        scales.append((cols, place, mean, inv_std, gain[:, place] * inv_std, shift[:, place]))

    def sums(of, added, incoming, result, cols, mean, scale, bias):
        centered = of[:, cols] - mean
        summed = centered * scale + bias + added.astype(f32)
        value = jnp.where(summed > 0.0, incoming.astype(f32), 0.0)
        result[:, cols] = value.astype(bf16)
        return (
            jnp.sum(value, axis=0, keepdims=True),
            jnp.sum(value * centered, axis=0, keepdims=True),
        )

    near_sums = [
        sums(conv, block[:, place], out[:, place], grad, cols, mean, scale, bias)
        for cols, place, mean, _, scale, bias in scales
    ]
    for load in loads:
        load.wait()
    for j, (cols, _, mean, inv_std, scale, bias) in enumerate(scales):
        sum_grad, sum_cross = sums(
            conv_other, block_other[:, cols], out_other[:, cols], grad_other, cols, mean, scale, bias
        )
        sum_grad += near_sums[j][0]
        sum_cross += near_sums[j][1]
        tile = jnp.concatenate(fold(sum_grad) + fold(sum_cross * inv_std), axis=0)
        stats[:, 8 * j : 8 * j + 8] = jnp.broadcast_to(tile[None], (stats.shape[0], 8, lanes))


def weight_kernel(
    sizes,
    conv,
    conv_other,
    moments,
    stats,
    gain,
    grad,
    grad_other,
    acts,
    acts_other,
    weight,
    act,
    act_other,
    squares,
    result_out,
    wide,
    acts_t,
    acts_t_other,
    grad_conv,
    grad_conv_other,
    out,
    sems,
):
    nx, nyl, nyh = sizes
    core = lax.axis_index("c")
    rows, half = conv.shape
    group_rows = 2 * rows * moments.shape[0]
    part = wide.shape[0] // (nyl * nyh)
    step = part // nx
    length = groups * nyh * step
    acts_t[...] = acts[...].T
    acts_t_other[...] = acts_other[...].T
    writes = []
    for j, cols in enumerate(columns(half)):
        place = pl.ds(pl.multiple_of(core * half + j * chunk, chunk), chunk)
        mean, inv_std = pooled(moments[:, 8 * j : 8 * j + 8], 2 * rows)
        sums = jnp.sum(stats[:, 8 * j : 8 * j + 8], axis=0)
        sum_grad, sum_cross = sums[:groups], sums[groups:]
        shift = unfold(sum_grad) / group_rows
        slope = inv_std * unfold(sum_cross) / group_rows
        scale = gain[:, place] * inv_std
        product = 0.0
        for of, pre, left, result in (
            (conv, grad, acts_t, grad_conv),
            (conv_other, grad_other, acts_t_other, grad_conv_other),
        ):
            value = pre[:, cols].astype(f32) - shift - (of[:, cols] - mean) * slope
            narrow = (scale * value).astype(bf16)
            result[:, cols] = narrow
            product += jnp.dot(left[...], narrow, preferred_element_type=f32)
        wide[...] = product
        planes = (*high_low(sum_grad), *high_low(sum_cross))
        for x in range(nx):
            last = jnp.concatenate(
                [planes[x] / (nyl * nyh), jnp.zeros((16 - groups, lanes), f32)], axis=0
            )
            for yl in range(nyl):
                piece = (j * nx + x) * nyl + yl
                rows_of = [
                    wide[
                        pl.ds((yh * nyl + yl) * part + step * x, step), pl.ds(q * lanes, lanes)
                    ]
                    for q in range(groups)
                    for yh in range(nyh)
                ]
                out[piece, :length] = jnp.concatenate(rows_of, axis=0).astype(bf16)
                out[piece, length:] = last.astype(bf16)
        ready = pl.ds(j * nx * nyl, nx * nyl)
        writes.append(pltpu.make_async_copy(out.at[ready], result_out.at[ready], sems.at[j]))
        writes[-1].start()

    dims = (((1,), (1,)), ((), ()))
    act[...] = lax.dot_general(grad_conv[...], weight[...], dims, preferred_element_type=f32)
    act_other[...] = lax.dot_general(
        grad_conv_other[...], weight[...], dims, preferred_element_type=f32
    ).astype(bf16)
    total = jnp.zeros((8, lanes), f32)
    for cols in columns(weight.shape[1]):
        value = weight[:, cols].astype(f32)
        total += sum(fold(jnp.sum((value * value).reshape(-1, 8, chunk), axis=0)))
    squares[...] = total
    for write in writes:
        write.wait()


def near_kernel(nyh, received, out, total):
    total[...] = jnp.sum(received[...].astype(f32), axis=0)
    length = total.shape[0] - 16
    step = length // (groups * nyh)
    tail = high_low(total[length : length + groups, :])
    for yh in range(nyh):
        starts = [(q * nyh + yh) * step for q in range(groups)]
        own = [total[at : at + step, :] for at in starts]
        tile = jnp.concatenate([*own, *tail], axis=0).astype(bf16)
        for zh in range(out.shape[0] // nyh):
            out[zh * nyh + yh] = tile


def far_kernel(received, out):
    total = jnp.sum(received[...].astype(f32), axis=0)
    at = total.shape[0] - 2 * groups
    value = total[:at]
    square = jnp.sum(jnp.sum(value * value, axis=0, keepdims=True), axis=1, keepdims=True)
    square = jnp.broadcast_to(square, (1, lanes))
    tail = total[at : at + groups] + total[at + groups :]
    tile = [value, *high_low(tail), *high_low(square), jnp.zeros((6, lanes), f32)]
    tile = jnp.concatenate(tile, axis=0).astype(bf16)
    out[...] = jnp.broadcast_to(tile[None], out.shape)


def places(parts, nx):
    for zl in range(parts.shape[0] // nx):
        values = [parts[zl * nx + x].astype(f32) for x in range(nx)]
        for q in range(groups):
            yield zl * nx, q, pl.ds((zl * groups + q) * lanes, lanes), values


def owned(parts, first, q, owner, count):
    values = [parts[first + owner * count + i].astype(f32) for i in range(count)]
    step = (values[0].shape[0] - 16) // groups
    return jnp.concatenate([v[q * step : (q + 1) * step] for v in values], axis=0)


def sums_of(values, q):
    at = values[0].shape[0] - 16 + q
    planes = [v[at : at + 1] + v[at + groups : at + groups + 1] for v in values]
    return planes[0] + planes[1], planes[2] + planes[3]


def split_kernel(nx, parts, weight_squares, theirs, squares):
    other = 1 - lax.axis_index("c")
    part = theirs.shape[0] - 8
    for first, q, cols, values in places(parts, nx):
        theirs[:part, cols] = owned(parts, first, q, other, nx // 2)
        shift, gain = sums_of(values, q)
        theirs[part:, cols] = jnp.concatenate([shift, gain, jnp.zeros((6, lanes), f32)], axis=0)
    total = jnp.sum(parts[...].astype(f32), axis=0)
    at = total.shape[0] - 8
    square = total[at : at + 1] + total[at + 1 : at + 2]
    weight_square = jnp.sum(weight_squares[...], axis=0, keepdims=True)
    weight_square = jnp.sum(weight_square, axis=1, keepdims=True)
    weight_square = jnp.broadcast_to(weight_square, (1, lanes))
    tile = jnp.concatenate([square, weight_square, jnp.zeros((6, lanes), f32)], axis=0)
    squares[...] = jnp.broadcast_to(tile[None], squares.shape)


def step_kernel(nx, parts, arrived, squares, weight, velocity, out, gain, shift):
    core = lax.axis_index("c")
    part, cout = out.shape
    half = cout // 2
    total = jnp.sum(squares[...], axis=0)
    grad_norm = jnp.sqrt(total[:1, :1])
    weight_norm = jnp.sqrt(total[1:2, :1] / (squares.shape[0] // 2))
    ratio = weight_norm / (grad_norm + weight_decay * weight_norm)

    def update(cols, weight_grad):
        decayed = weight_grad + weight_decay * weight[:, cols].astype(f32)
        out[:, cols] = momentum * velocity[:, cols] + ratio * decayed

    for first, q, cols, values in places(parts, nx):
        here = pl.ds(pl.multiple_of(core * half + cols.start, lanes), lanes)
        there = pl.ds(pl.multiple_of((1 - core) * half + cols.start, lanes), lanes)
        update(here, owned(parts, first, q, core, nx // 2))
        update(there, arrived[:part, cols])
        shift[:, here], gain[:, here] = sums_of(values, q)
        last = arrived[part:, cols]
        shift[:, there], gain[:, there] = last[:1], last[1:2]


def shape(dims, dtype):
    return jax.ShapeDtypeStruct(dims, dtype)


def whole(dims):
    return pl.BlockSpec(dims, lambda j: (0,) * len(dims))


def params(mib=24):
    return pltpu.CompilerParams(vmem_limit_bytes=mib << 20)


def call(kernel, name, operands, outs, scratch=(), loaded=0, written=None):
    anywhere = pl.BlockSpec(memory_space=pl.ANY)
    at = len(operands) - loaded
    in_specs = [whole(value.shape) for value in operands[:at]] + [anywhere] * loaded
    out_specs = [whole(out.shape) for out in outs]
    if written is not None:
        out_specs.append(anywhere)
        outs = [*outs, pltpu.HBM(written.shape, written.dtype)]
    return pl.pallas_call(
        kernel,
        grid=(1,),
        in_specs=in_specs,
        out_specs=out_specs,
        out_shape=outs,
        scratch_shapes=scratch,
        compiler_params=params(),
        name=name,
    )(*operands)


def local(block_input, activations, conv_weight, bn_gain, bn_shift, out_grad, velocity):
    rows, cin = activations.shape
    part, cout = conv_weight.shape
    half = cout // 2
    nzh, nzl, nx = (lax.axis_size(a) for a in rep)
    nyh, nyl = (lax.axis_size(a) for a in y_axes)
    ny = nyh * nyl
    members = 2 * ny
    first_core = lax.axis_index("c") == 0
    gain, shift = bn_gain.reshape(1, cout), bn_shift.reshape(1, cout)

    def other_half(value):
        return jnp.where(first_core, value[:, half:], value[:, :half])

    (pieces,) = call(
        pieces_kernel,
        "pieces",
        (conv_weight,),
        [],
        [pltpu.SemaphoreType.DMA((members,))],
        loaded=1,
        written=shape((members, part, half), bf16),
    )
    weight = exchange(pieces, bn).reshape(cin, half)
    acts_other = swap(activations)
    block_other = swap(other_half(block_input))
    out_other = swap(other_half(out_grad))
    weight, acts_other = lax.optimization_barrier((weight, acts_other))

    wide = shape((rows, half), f32)
    narrow = shape((rows, half), bf16)
    sums = shape((ny, 2 * half // lanes, lanes), f32)
    conv, conv_other, moments = call(
        moments_kernel, "moments", (activations, acts_other, weight), [wide, wide, sums]
    )
    moments, block_other, out_other = lax.optimization_barrier((moments, block_other, out_other))
    moments = exchange(moments, y_axes)
    grad, grad_other, stats = call(
        stats_kernel,
        "stats",
        (conv, conv_other, moments, gain, shift, block_input, out_grad, block_other, out_other),
        [narrow, narrow, sums],
        [pltpu.VMEM((rows, half), bf16)] * 2 + [pltpu.SemaphoreType.DMA((2,))],
        loaded=2,
    )
    stats = exchange(stats, y_axes)
    count = nzl * nx * nyl
    step = 2 * part // nx
    length = groups * nyh * step
    act, act_other, weight_squares, partial = call(
        functools.partial(weight_kernel, (nx, nyl, nyh)),
        "weight_partial",
        (conv, conv_other, moments, stats, gain, grad, grad_other, activations, acts_other, weight),
        [shape((rows, cin), f32), shape((rows, cin), bf16), shape((8, lanes), f32)],
        [pltpu.VMEM((cin, chunk), f32)]
        + [pltpu.VMEM((cin, rows), bf16)] * 2
        + [pltpu.VMEM((rows, half), bf16)] * 2
        + [pltpu.VMEM((count, length + 16, lanes), bf16)]
        + [pltpu.SemaphoreType.DMA((half // chunk,))],
        written=shape((count, length + 16, lanes), bf16),
    )
    act_grad = (act + swap(act_other).astype(f32)).astype(bf16)
    partial, act_grad = lax.optimization_barrier((exchange(partial, near), act_grad))

    (partial,) = call(
        functools.partial(near_kernel, nyh),
        "near_sum",
        (partial,),
        [shape((nzh * nyh, groups * (step + 2), lanes), bf16)],
        [pltpu.VMEM((length + 16, lanes), f32)],
    )
    (ready,) = call(
        far_kernel,
        "far_sum",
        (exchange(partial, far),),
        [shape((nzl * nx, groups * step + 16, lanes), bf16)],
    )
    ready = exchange(ready, ("zl", "x"))
    theirs, squares = call(
        functools.partial(split_kernel, nx),
        "split",
        (ready, weight_squares),
        [shape((part + 8, half), f32), shape((members, 8, lanes), f32)],
    )
    arrived = swap(theirs)
    squares = exchange(squares, bn)
    new_velocity, gain_grad, shift_grad = call(
        functools.partial(step_kernel, nx),
        "step",
        (ready, arrived, squares, conv_weight, velocity),
        [shape((part, cout), f32), shape((1, cout), f32), shape((1, cout), f32)],
    )
    return (act_grad, gain_grad.reshape(cout), shift_grad.reshape(cout), new_velocity)


def solution(mesh, dims=(4, 2, 4, 4, 2, 2)):
    fine = Mesh(mesh.devices.reshape(dims), rep + bn)
    every = P(rep + bn, None)
    return jax.shard_map(
        local,
        mesh=fine,
        in_specs=(every, every, P(bn, None), P(), P(), every, P(bn, None)),
        out_specs=(every, P(), P(), P(bn, None)),
        check_vma=False,
    )
```

```python
import functools

import jax
import jax.numpy as jnp
from jax import lax
from jax.experimental import pallas as pl
from jax.experimental.pallas import tpu as pltpu
from jax.sharding import Mesh, PartitionSpec as P

epsilon = 1e-05
weight_decay = 5e-05
momentum = 0.9
f32, bf16 = jnp.float32, jnp.bfloat16
rep = ("zh", "zl", "x")
y_axes = ("yh", "yl")
bn = ("yh", "yl", "c")
near = ("zl", "x", "yl")
far = ("zh", "yh")
lanes = 128
chunk = 512
groups = chunk // lanes


def swap(value):
    return lax.ppermute(value, "c", [(0, 1), (1, 0)])


def exchange(pieces, axis):
    return lax.all_to_all(pieces, axis, 0, 0, tiled=True)


def copies(value, axis):
    n = lax.axis_size(axis)
    return exchange(jnp.broadcast_to(value[None], (n, *value.shape)), axis)


def fold(row):
    return [row[:, q * lanes : (q + 1) * lanes] for q in range(groups)]


def unfold(tile):
    return jnp.concatenate([tile[q : q + 1] for q in range(groups)], axis=1)


def high_low(value):
    high = value.astype(bf16).astype(f32)
    return high, value - high


def columns(width):
    return [pl.ds(start, chunk) for start in range(0, width, chunk)]


def eighth_kernel(nx, weight, out):
    half = weight.shape[1] // 2
    place = lax.axis_index("zl") * nx + lax.axis_index("x")
    for c in range(2):
        tile = weight[:, pl.ds(pl.multiple_of(c * half + place * lanes, lanes), lanes)]
        for y in range(out.shape[0] // 2):
            out[2 * y + c] = tile


def copies_kernel(block, out, sems):
    writes = [pltpu.make_async_copy(block, out.at[i], sems.at[i]) for i in range(out.shape[0])]
    for write in writes:
        write.start()
    for write in writes:
        write.wait()


def moments_kernel(acts, acts_other, parts, weight, conv, conv_other, moments):
    for i in range(parts.shape[0]):
        weight[:, i * lanes : (i + 1) * lanes] = parts[i]
    count = 2 * conv.shape[0]
    for j, cols in enumerate(columns(conv.shape[1])):
        both = []
        for rows, out in ((acts, conv), (acts_other, conv_other)):
            value = jnp.dot(rows[...], weight[:, cols], preferred_element_type=f32)
            out[:, cols] = value
            both.append(value)
        mean = sum(jnp.sum(value, axis=0, keepdims=True) for value in both) / count
        square = sum(jnp.sum((v - mean) * (v - mean), axis=0, keepdims=True) for v in both)
        tile = jnp.concatenate(fold(mean) + fold(square), axis=0)
        moments[:, 8 * j : 8 * j + 8] = jnp.broadcast_to(tile[None], (moments.shape[0], 8, lanes))


def pooled(moments, rows):
    members = moments.shape[0]
    means, squares = moments[:, :groups], moments[:, groups:]
    mean = jnp.sum(means, axis=0) / members
    offset = means - mean[None]
    square = jnp.sum(squares, axis=0) + rows * jnp.sum(offset * offset, axis=0)
    inv_std = lax.rsqrt(square / (rows * members) + epsilon)
    return unfold(mean), unfold(inv_std)


def stats_kernel(
    conv,
    conv_other,
    moments,
    gain,
    shift,
    block,
    out,
    block_far,
    out_far,
    grad,
    grad_other,
    stats,
    block_other,
    out_other,
    sems,
):
    rows, half = conv.shape
    core = lax.axis_index("c")
    loads = [
        pltpu.make_async_copy(block_far, block_other, sems.at[0]),
        pltpu.make_async_copy(out_far, out_other, sems.at[1]),
    ]
    for load in loads:
        load.start()
    scales = []
    for j, cols in enumerate(columns(half)):
        place = pl.ds(pl.multiple_of(core * half + j * chunk, chunk), chunk)
        mean, inv_std = pooled(moments[:, 8 * j : 8 * j + 8], 2 * rows)
        scales.append((cols, place, mean, inv_std, gain[:, place] * inv_std, shift[:, place]))

    def sums(of, added, incoming, result, cols, mean, scale, bias):
        centered = of[:, cols] - mean
        summed = centered * scale + bias + added.astype(f32)
        value = jnp.where(summed > 0.0, incoming.astype(f32), 0.0)
        result[:, cols] = value.astype(bf16)
        return (
            jnp.sum(value, axis=0, keepdims=True),
            jnp.sum(value * centered, axis=0, keepdims=True),
        )

    near_sums = [
        sums(conv, block[:, place], out[:, place], grad, cols, mean, scale, bias)
        for cols, place, mean, _, scale, bias in scales
    ]
    for load in loads:
        load.wait()
    for j, (cols, _, mean, inv_std, scale, bias) in enumerate(scales):
        sum_grad, sum_cross = sums(
            conv_other, block_other[:, cols], out_other[:, cols], grad_other, cols, mean, scale, bias
        )
        sum_grad += near_sums[j][0]
        sum_cross += near_sums[j][1]
        tile = jnp.concatenate(fold(sum_grad) + fold(sum_cross * inv_std), axis=0)
        stats[:, 8 * j : 8 * j + 8] = jnp.broadcast_to(tile[None], (stats.shape[0], 8, lanes))


def weight_kernel(
    sizes,
    conv,
    conv_other,
    moments,
    stats,
    gain,
    grad,
    grad_other,
    acts,
    acts_other,
    weight,
    act,
    act_other,
    squares,
    result_out,
    wide,
    acts_t,
    acts_t_other,
    grad_conv,
    grad_conv_other,
    out,
    sems,
):
    nx, nyl, nyh = sizes
    core = lax.axis_index("c")
    rows, half = conv.shape
    group_rows = 2 * rows * moments.shape[0]
    part = wide.shape[0] // (nyl * nyh)
    step = part // nx
    length = groups * nyh * step
    acts_t[...] = acts[...].T
    acts_t_other[...] = acts_other[...].T
    writes = []
    for j, cols in enumerate(columns(half)):
        place = pl.ds(pl.multiple_of(core * half + j * chunk, chunk), chunk)
        mean, inv_std = pooled(moments[:, 8 * j : 8 * j + 8], 2 * rows)
        sums = jnp.sum(stats[:, 8 * j : 8 * j + 8], axis=0)
        sum_grad, sum_cross = sums[:groups], sums[groups:]
        shift = unfold(sum_grad) / group_rows
        slope = inv_std * unfold(sum_cross) / group_rows
        scale = gain[:, place] * inv_std
        product = 0.0
        for of, pre, left, result in (
            (conv, grad, acts_t, grad_conv),
            (conv_other, grad_other, acts_t_other, grad_conv_other),
        ):
            value = pre[:, cols].astype(f32) - shift - (of[:, cols] - mean) * slope
            narrow = (scale * value).astype(bf16)
            result[:, cols] = narrow
            product += jnp.dot(left[...], narrow, preferred_element_type=f32)
        wide[...] = product
        planes = (*high_low(sum_grad), *high_low(sum_cross))
        for x in range(nx):
            last = jnp.concatenate(
                [planes[x] / (nyl * nyh), jnp.zeros((16 - groups, lanes), f32)], axis=0
            )
            for yl in range(nyl):
                piece = (j * nx + x) * nyl + yl
                rows_of = [
                    wide[
                        pl.ds((yh * nyl + yl) * part + step * x, step), pl.ds(q * lanes, lanes)
                    ]
                    for q in range(groups)
                    for yh in range(nyh)
                ]
                out[piece, :length] = jnp.concatenate(rows_of, axis=0).astype(bf16)
                out[piece, length:] = last.astype(bf16)
        ready = pl.ds(j * nx * nyl, nx * nyl)
        writes.append(pltpu.make_async_copy(out.at[ready], result_out.at[ready], sems.at[j]))
        writes[-1].start()

    dims = (((1,), (1,)), ((), ()))
    act[...] = lax.dot_general(grad_conv[...], weight[...], dims, preferred_element_type=f32)
    act_other[...] = lax.dot_general(
        grad_conv_other[...], weight[...], dims, preferred_element_type=f32
    ).astype(bf16)
    total = jnp.zeros((8, lanes), f32)
    for cols in columns(weight.shape[1]):
        value = weight[:, cols].astype(f32)
        total += sum(fold(jnp.sum((value * value).reshape(-1, 8, chunk), axis=0)))
    squares[...] = total
    for write in writes:
        write.wait()


def near_kernel(nyh, received, out, total):
    total[...] = jnp.sum(received[...].astype(f32), axis=0)
    length = total.shape[0] - 16
    step = length // (groups * nyh)
    tail = high_low(total[length : length + groups, :])
    for yh in range(nyh):
        starts = [(q * nyh + yh) * step for q in range(groups)]
        own = [total[at : at + step, :] for at in starts]
        tile = jnp.concatenate([*own, *tail], axis=0).astype(bf16)
        for zh in range(out.shape[0] // nyh):
            out[zh * nyh + yh] = tile


def spread(value):
    value = jnp.sum(jnp.sum(value, axis=0, keepdims=True), axis=1, keepdims=True)
    return jnp.broadcast_to(value, (1, lanes))


def far_kernel(received, weight_squares, out):
    total = jnp.sum(received[...].astype(f32), axis=0)
    at = total.shape[0] - 2 * groups
    value = total[:at]
    tail = total[at : at + groups] + total[at + groups :]
    square, weight_square = spread(value * value), spread(weight_squares[...])
    last = [*high_low(square), *high_low(weight_square), jnp.zeros((4, lanes), f32)]
    tile = jnp.concatenate([value, *high_low(tail), *last], axis=0).astype(bf16)
    out[...] = jnp.broadcast_to(tile[None], out.shape)


def squares_kernel(parts, squares):
    total = jnp.sum(parts[...].astype(f32), axis=0)
    at = total.shape[0] - 8
    square = total[at : at + 1] + total[at + 1 : at + 2]
    weight_square = (total[at + 2 : at + 3] + total[at + 3 : at + 4]) / (parts.shape[0] // 2)
    tile = jnp.concatenate([square, weight_square, jnp.zeros((6, lanes), f32)], axis=0)
    squares[...] = jnp.broadcast_to(tile[None], squares.shape)


def step_kernel(nx, parts, squares, weight, velocity, out, gain, shift):
    core = lax.axis_index("c")
    half = out.shape[1] // 2
    total = jnp.sum(squares[...], axis=0)
    grad_norm = jnp.sqrt(total[:1, :1])
    weight_norm = jnp.sqrt(total[1:2, :1] / squares.shape[0])
    ratio = weight_norm / (grad_norm + weight_decay * weight_norm)
    count = nx // 2
    for zl in range(parts.shape[0] // (2 * nx)):
        for c in range(2):
            values = [parts[(zl * nx + x) * 2 + c].astype(f32) for x in range(nx)]
            own = [
                parts[(zl * nx + core * count + i) * 2 + c].astype(f32) for i in range(count)
            ]
            step = (own[0].shape[0] - 16) // groups
            for q in range(groups):
                cols = pl.ds(c * half + (zl * groups + q) * lanes, lanes)
                weight_grad = jnp.concatenate([v[q * step : (q + 1) * step] for v in own], axis=0)
                decayed = weight_grad + weight_decay * weight[:, cols].astype(f32)
                out[:, cols] = momentum * velocity[:, cols] + ratio * decayed
                at = groups * step + q
                planes = [v[at : at + 1] + v[at + groups : at + groups + 1] for v in values]
                shift[:, cols] = planes[0] + planes[1]
                gain[:, cols] = planes[2] + planes[3]


def shape(dims, dtype):
    return jax.ShapeDtypeStruct(dims, dtype)


def whole(dims):
    return pl.BlockSpec(dims, lambda j: (0,) * len(dims))


def params(mib=24):
    return pltpu.CompilerParams(vmem_limit_bytes=mib << 20)


def call(kernel, name, operands, outs, scratch=(), loaded=0, written=None):
    anywhere = pl.BlockSpec(memory_space=pl.ANY)
    at = len(operands) - loaded
    in_specs = [whole(value.shape) for value in operands[:at]] + [anywhere] * loaded
    out_specs = [whole(out.shape) for out in outs]
    if written is not None:
        out_specs.append(anywhere)
        outs = [*outs, pltpu.HBM(written.shape, written.dtype)]
    return pl.pallas_call(
        kernel,
        grid=(1,),
        in_specs=in_specs,
        out_specs=out_specs,
        out_shape=outs,
        scratch_shapes=scratch,
        compiler_params=params(),
        name=name,
    )(*operands)


def local(block_input, activations, conv_weight, bn_gain, bn_shift, out_grad, velocity):
    rows, cin = activations.shape
    part, cout = conv_weight.shape
    half = cout // 2
    nzh, nzl, nx = (lax.axis_size(a) for a in rep)
    nyh, nyl = (lax.axis_size(a) for a in y_axes)
    ny = nyh * nyl
    members = 2 * ny
    first_core = lax.axis_index("c") == 0
    gain, shift = bn_gain.reshape(1, cout), bn_shift.reshape(1, cout)

    def other_half(value):
        return jnp.where(first_core, value[:, half:], value[:, :half])

    (eighth,) = call(
        functools.partial(eighth_kernel, nx),
        "eighth",
        (conv_weight,),
        [shape((members, part, lanes), bf16)],
    )
    eighth = exchange(eighth, bn).reshape(cin, lanes)
    (spread_out,) = call(
        copies_kernel,
        "weight_copies",
        (eighth,),
        [],
        [pltpu.SemaphoreType.DMA((nzl * nx,))],
        written=shape((nzl * nx, cin, lanes), bf16),
    )
    weight_parts = exchange(spread_out, ("zl", "x"))
    acts_other = swap(activations)
    block_other = swap(other_half(block_input))
    out_other = swap(other_half(out_grad))
    weight_parts, acts_other = lax.optimization_barrier((weight_parts, acts_other))

    wide = shape((rows, half), f32)
    narrow = shape((rows, half), bf16)
    sums = shape((ny, 2 * half // lanes, lanes), f32)
    weight, conv, conv_other, moments = call(
        moments_kernel,
        "moments",
        (activations, acts_other, weight_parts),
        [shape((cin, half), bf16), wide, wide, sums],
    )
    moments, block_other, out_other = lax.optimization_barrier((moments, block_other, out_other))
    moments = exchange(moments, y_axes)
    grad, grad_other, stats = call(
        stats_kernel,
        "stats",
        (conv, conv_other, moments, gain, shift, block_input, out_grad, block_other, out_other),
        [narrow, narrow, sums],
        [pltpu.VMEM((rows, half), bf16)] * 2 + [pltpu.SemaphoreType.DMA((2,))],
        loaded=2,
    )
    stats = exchange(stats, y_axes)
    count = nzl * nx * nyl
    step = 2 * part // nx
    length = groups * nyh * step
    act, act_other, weight_squares, partial = call(
        functools.partial(weight_kernel, (nx, nyl, nyh)),
        "weight_partial",
        (conv, conv_other, moments, stats, gain, grad, grad_other, activations, acts_other, weight),
        [shape((rows, cin), f32), shape((rows, cin), bf16), shape((8, lanes), f32)],
        [pltpu.VMEM((cin, chunk), f32)]
        + [pltpu.VMEM((cin, rows), bf16)] * 2
        + [pltpu.VMEM((rows, half), bf16)] * 2
        + [pltpu.VMEM((count, length + 16, lanes), bf16)]
        + [pltpu.SemaphoreType.DMA((half // chunk,))],
        written=shape((count, length + 16, lanes), bf16),
    )
    act_grad = (act + swap(act_other).astype(f32)).astype(bf16)
    partial, act_grad = lax.optimization_barrier((exchange(partial, near), act_grad))

    (partial,) = call(
        functools.partial(near_kernel, nyh),
        "near_sum",
        (partial,),
        [shape((nzh * nyh, groups * (step + 2), lanes), bf16)],
        [pltpu.VMEM((length + 16, lanes), f32)],
    )
    (ready,) = call(
        far_kernel,
        "far_sum",
        (exchange(partial, far), weight_squares),
        [shape((2 * nzl * nx, groups * step + 16, lanes), bf16)],
    )
    ready = exchange(ready, ("zl", "x", "c"))
    (squares,) = call(squares_kernel, "squares", (ready,), [shape((ny, 8, lanes), f32)])
    squares = exchange(squares, y_axes)
    new_velocity, gain_grad, shift_grad = call(
        functools.partial(step_kernel, nx),
        "step",
        (ready, squares, conv_weight, velocity),
        [shape((part, cout), f32), shape((1, cout), f32), shape((1, cout), f32)],
    )
    return (act_grad, gain_grad.reshape(cout), shift_grad.reshape(cout), new_velocity)


def solution(mesh, dims=(4, 2, 4, 4, 2, 2)):
    fine = Mesh(mesh.devices.reshape(dims), rep + bn)
    every = P(rep + bn, None)
    return jax.shard_map(
        local,
        mesh=fine,
        in_specs=(every, every, P(bn, None), P(), P(), every, P(bn, None)),
        out_specs=(every, P(), P(), P(bn, None)),
        check_vma=False,
    )
```

```python
import functools

import jax
import jax.numpy as jnp
from jax import lax
from jax.experimental import pallas as pl
from jax.experimental.pallas import tpu as pltpu
from jax.sharding import Mesh, PartitionSpec as P

epsilon = 1e-05
weight_decay = 5e-05
momentum = 0.9
f32, bf16 = jnp.float32, jnp.bfloat16
rep = ("zh", "zl", "x")
y_axes = ("yh", "yl")
bn = ("yh", "yl", "c")
near = ("zl", "x", "yl")
far = ("zh", "yh")
lanes = 128
chunk = 512
groups = chunk // lanes


def swap(value):
    return lax.ppermute(value, "c", [(0, 1), (1, 0)])


def exchange(pieces, axis):
    return lax.all_to_all(pieces, axis, 0, 0, tiled=True)


def copies(value, axis):
    n = lax.axis_size(axis)
    return exchange(jnp.broadcast_to(value[None], (n, *value.shape)), axis)


def fold(row):
    return [row[:, q * lanes : (q + 1) * lanes] for q in range(groups)]


def unfold(tile):
    return jnp.concatenate([tile[q : q + 1] for q in range(groups)], axis=1)


def high_low(value):
    high = value.astype(bf16).astype(f32)
    return high, value - high


def columns(width):
    return [pl.ds(start, chunk) for start in range(0, width, chunk)]


def eighth_kernel(nx, weight, out):
    half = weight.shape[1] // 2
    place = lax.axis_index("zl") * nx + lax.axis_index("x")
    for c in range(2):
        tile = weight[:, pl.ds(pl.multiple_of(c * half + place * lanes, lanes), lanes)]
        for y in range(out.shape[0] // 2):
            out[2 * y + c] = tile


def copies_kernel(block, out, sems):
    writes = [pltpu.make_async_copy(block, out.at[i], sems.at[i]) for i in range(out.shape[0])]
    for write in writes:
        write.start()
    for write in writes:
        write.wait()


def moments_kernel(acts, acts_other, parts, weight, conv, conv_other, moments):
    for i in range(parts.shape[0]):
        weight[:, i * lanes : (i + 1) * lanes] = parts[i]
    count = 2 * conv.shape[0]
    for j, cols in enumerate(columns(conv.shape[1])):
        both = []
        for rows, out in ((acts, conv), (acts_other, conv_other)):
            value = jnp.dot(rows[...], weight[:, cols], preferred_element_type=f32)
            out[:, cols] = value
            both.append(value)
        mean = sum(jnp.sum(value, axis=0, keepdims=True) for value in both) / count
        square = sum(jnp.sum((v - mean) * (v - mean), axis=0, keepdims=True) for v in both)
        tile = jnp.concatenate(fold(mean) + fold(square), axis=0)
        moments[:, 8 * j : 8 * j + 8] = jnp.broadcast_to(tile[None], (moments.shape[0], 8, lanes))


def pooled(moments, rows):
    members = moments.shape[0]
    means, squares = moments[:, :groups], moments[:, groups:]
    mean = jnp.sum(means, axis=0) / members
    offset = means - mean[None]
    square = jnp.sum(squares, axis=0) + rows * jnp.sum(offset * offset, axis=0)
    inv_std = lax.rsqrt(square / (rows * members) + epsilon)
    return unfold(mean), unfold(inv_std)


def stats_kernel(
    conv,
    conv_other,
    moments,
    gain,
    shift,
    block_in,
    out_in,
    block_far,
    out_far,
    grad,
    grad_other,
    stats,
    block,
    out,
    block_other,
    out_other,
    sems,
):
    rows, half = conv.shape
    core = lax.axis_index("c")
    loads = [
        pltpu.make_async_copy(block_in, block, sems.at[0]),
        pltpu.make_async_copy(out_in, out, sems.at[1]),
        pltpu.make_async_copy(block_far, block_other, sems.at[2]),
        pltpu.make_async_copy(out_far, out_other, sems.at[3]),
    ]
    for load in loads:
        load.start()
    scales = []
    for j, cols in enumerate(columns(half)):
        place = pl.ds(pl.multiple_of(core * half + j * chunk, chunk), chunk)
        mean, inv_std = pooled(moments[:, 8 * j : 8 * j + 8], 2 * rows)
        scales.append((cols, mean, inv_std, gain[:, place] * inv_std, shift[:, place]))

    def sums(of, added, incoming, result, cols, mean, scale, bias):
        centered = of[:, cols] - mean
        summed = centered * scale + bias + added.astype(f32)
        value = jnp.where(summed > 0.0, incoming.astype(f32), 0.0)
        result[:, cols] = value.astype(bf16)
        return (
            jnp.sum(value, axis=0, keepdims=True),
            jnp.sum(value * centered, axis=0, keepdims=True),
        )

    for load in loads[:2]:
        load.wait()
    near_sums = [
        sums(conv, block[:, cols], out[:, cols], grad, cols, mean, scale, bias)
        for cols, mean, _, scale, bias in scales
    ]
    for load in loads[2:]:
        load.wait()
    for j, (cols, mean, inv_std, scale, bias) in enumerate(scales):
        sum_grad, sum_cross = sums(
            conv_other, block_other[:, cols], out_other[:, cols], grad_other, cols, mean, scale, bias
        )
        sum_grad += near_sums[j][0]
        sum_cross += near_sums[j][1]
        tile = jnp.concatenate(fold(sum_grad) + fold(sum_cross * inv_std), axis=0)
        stats[:, 8 * j : 8 * j + 8] = jnp.broadcast_to(tile[None], (stats.shape[0], 8, lanes))


def weight_kernel(
    sizes,
    conv,
    conv_other,
    moments,
    stats,
    gain,
    grad,
    grad_other,
    acts,
    acts_other,
    weight,
    act,
    act_other,
    squares,
    result_out,
    wide,
    acts_t,
    acts_t_other,
    grad_conv,
    grad_conv_other,
    out,
    sems,
):
    nx, nyl, nyh = sizes
    core = lax.axis_index("c")
    rows, half = conv.shape
    group_rows = 2 * rows * moments.shape[0]
    part = wide.shape[0] // (nyl * nyh)
    step = part // nx
    length = groups * nyh * step
    acts_t[...] = acts[...].T
    acts_t_other[...] = acts_other[...].T
    writes = []
    for j, cols in enumerate(columns(half)):
        place = pl.ds(pl.multiple_of(core * half + j * chunk, chunk), chunk)
        mean, inv_std = pooled(moments[:, 8 * j : 8 * j + 8], 2 * rows)
        sums = jnp.sum(stats[:, 8 * j : 8 * j + 8], axis=0)
        sum_grad, sum_cross = sums[:groups], sums[groups:]
        shift = unfold(sum_grad) / group_rows
        slope = inv_std * unfold(sum_cross) / group_rows
        scale = gain[:, place] * inv_std
        product = 0.0
        for of, pre, left, result in (
            (conv, grad, acts_t, grad_conv),
            (conv_other, grad_other, acts_t_other, grad_conv_other),
        ):
            value = pre[:, cols].astype(f32) - shift - (of[:, cols] - mean) * slope
            narrow = (scale * value).astype(bf16)
            result[:, cols] = narrow
            product += jnp.dot(left[...], narrow, preferred_element_type=f32)
        wide[...] = product
        planes = (*high_low(sum_grad), *high_low(sum_cross))
        for x in range(nx):
            last = jnp.concatenate(
                [planes[x] / (nyl * nyh), jnp.zeros((16 - groups, lanes), f32)], axis=0
            )
            for yl in range(nyl):
                piece = (j * nx + x) * nyl + yl
                rows_of = [
                    wide[
                        pl.ds((yh * nyl + yl) * part + step * x, step), pl.ds(q * lanes, lanes)
                    ]
                    for q in range(groups)
                    for yh in range(nyh)
                ]
                out[piece, :length] = jnp.concatenate(rows_of, axis=0).astype(bf16)
                out[piece, length:] = last.astype(bf16)
        ready = pl.ds(j * nx * nyl, nx * nyl)
        writes.append(pltpu.make_async_copy(out.at[ready], result_out.at[ready], sems.at[j]))
        writes[-1].start()

    dims = (((1,), (1,)), ((), ()))
    act[...] = lax.dot_general(grad_conv[...], weight[...], dims, preferred_element_type=f32)
    act_other[...] = lax.dot_general(
        grad_conv_other[...], weight[...], dims, preferred_element_type=f32
    ).astype(bf16)
    total = jnp.zeros((8, lanes), f32)
    for cols in columns(weight.shape[1]):
        value = weight[:, cols].astype(f32)
        total += sum(fold(jnp.sum((value * value).reshape(-1, 8, chunk), axis=0)))
    squares[...] = total
    for write in writes:
        write.wait()


def near_kernel(nyh, received, out, total):
    total[...] = jnp.sum(received[...].astype(f32), axis=0)
    length = total.shape[0] - 16
    step = length // (groups * nyh)
    tail = high_low(total[length : length + groups, :])
    for yh in range(nyh):
        starts = [(q * nyh + yh) * step for q in range(groups)]
        own = [total[at : at + step, :] for at in starts]
        tile = jnp.concatenate([*own, *tail], axis=0).astype(bf16)
        for zh in range(out.shape[0] // nyh):
            out[zh * nyh + yh] = tile


def spread(value):
    value = jnp.sum(jnp.sum(value, axis=0, keepdims=True), axis=1, keepdims=True)
    return jnp.broadcast_to(value, (1, lanes))


def far_kernel(received, weight_squares, out):
    total = jnp.sum(received[...].astype(f32), axis=0)
    at = total.shape[0] - 2 * groups
    value = total[:at]
    tail = total[at : at + groups] + total[at + groups :]
    square, weight_square = spread(value * value), spread(weight_squares[...])
    last = [*high_low(square), *high_low(weight_square), jnp.zeros((4, lanes), f32)]
    tile = jnp.concatenate([value, *high_low(tail), *last], axis=0).astype(bf16)
    out[...] = jnp.broadcast_to(tile[None], out.shape)


def squares_kernel(parts, squares):
    total = jnp.sum(parts[...].astype(f32), axis=0)
    at = total.shape[0] - 8
    square = total[at : at + 1] + total[at + 1 : at + 2]
    weight_square = (total[at + 2 : at + 3] + total[at + 3 : at + 4]) / (parts.shape[0] // 2)
    tile = jnp.concatenate([square, weight_square, jnp.zeros((6, lanes), f32)], axis=0)
    squares[...] = jnp.broadcast_to(tile[None], squares.shape)


def step_kernel(nx, parts, squares, weight, velocity, out, gain, shift):
    core = lax.axis_index("c")
    half = out.shape[1] // 2
    total = jnp.sum(squares[...], axis=0)
    grad_norm = jnp.sqrt(total[:1, :1])
    weight_norm = jnp.sqrt(total[1:2, :1] / squares.shape[0])
    ratio = weight_norm / (grad_norm + weight_decay * weight_norm)
    count = nx // 2
    for zl in range(parts.shape[0] // (2 * nx)):
        for c in range(2):
            values = [parts[(zl * nx + x) * 2 + c].astype(f32) for x in range(nx)]
            own = [
                parts[(zl * nx + core * count + i) * 2 + c].astype(f32) for i in range(count)
            ]
            step = (own[0].shape[0] - 16) // groups
            for q in range(groups):
                cols = pl.ds(c * half + (zl * groups + q) * lanes, lanes)
                weight_grad = jnp.concatenate([v[q * step : (q + 1) * step] for v in own], axis=0)
                decayed = weight_grad + weight_decay * weight[:, cols].astype(f32)
                out[:, cols] = momentum * velocity[:, cols] + ratio * decayed
                at = groups * step + q
                planes = [v[at : at + 1] + v[at + groups : at + groups + 1] for v in values]
                shift[:, cols] = planes[0] + planes[1]
                gain[:, cols] = planes[2] + planes[3]


def shape(dims, dtype):
    return jax.ShapeDtypeStruct(dims, dtype)


def whole(dims):
    return pl.BlockSpec(dims, lambda j: (0,) * len(dims))


def params(mib=24):
    return pltpu.CompilerParams(vmem_limit_bytes=mib << 20)


def call(kernel, name, operands, outs, scratch=(), loaded=0, written=None):
    anywhere = pl.BlockSpec(memory_space=pl.ANY)
    at = len(operands) - loaded
    in_specs = [whole(value.shape) for value in operands[:at]] + [anywhere] * loaded
    out_specs = [whole(out.shape) for out in outs]
    if written is not None:
        out_specs.append(anywhere)
        outs = [*outs, pltpu.HBM(written.shape, written.dtype)]
    return pl.pallas_call(
        kernel,
        grid=(1,),
        in_specs=in_specs,
        out_specs=out_specs,
        out_shape=outs,
        scratch_shapes=scratch,
        compiler_params=params(),
        name=name,
    )(*operands)


def local(block_input, activations, conv_weight, bn_gain, bn_shift, out_grad, velocity):
    rows, cin = activations.shape
    part, cout = conv_weight.shape
    half = cout // 2
    nzh, nzl, nx = (lax.axis_size(a) for a in rep)
    nyh, nyl = (lax.axis_size(a) for a in y_axes)
    ny = nyh * nyl
    members = 2 * ny
    first_core = lax.axis_index("c") == 0
    gain, shift = bn_gain.reshape(1, cout), bn_shift.reshape(1, cout)

    def halves(value):
        low, high = value[:, :half], value[:, half:]
        return jnp.where(first_core, low, high), jnp.where(first_core, high, low)

    (eighth,) = call(
        functools.partial(eighth_kernel, nx),
        "eighth",
        (conv_weight,),
        [shape((members, part, lanes), bf16)],
    )
    eighth = exchange(eighth, bn).reshape(cin, lanes)
    (spread_out,) = call(
        copies_kernel,
        "weight_copies",
        (eighth,),
        [],
        [pltpu.SemaphoreType.DMA((nzl * nx,))],
        written=shape((nzl * nx, cin, lanes), bf16),
    )
    weight_parts = exchange(spread_out, ("zl", "x"))
    acts_other = swap(activations)
    block, block_other = halves(block_input)
    out, out_other = halves(out_grad)
    block_other, out_other = swap(block_other), swap(out_other)
    weight_parts, acts_other, block, out = lax.optimization_barrier(
        (weight_parts, acts_other, block, out)
    )

    wide = shape((rows, half), f32)
    narrow = shape((rows, half), bf16)
    sums = shape((ny, 2 * half // lanes, lanes), f32)
    weight, conv, conv_other, moments = call(
        moments_kernel,
        "moments",
        (activations, acts_other, weight_parts),
        [shape((cin, half), bf16), wide, wide, sums],
    )
    moments, block_other, out_other = lax.optimization_barrier((moments, block_other, out_other))
    moments = exchange(moments, y_axes)
    grad, grad_other, stats = call(
        stats_kernel,
        "stats",
        (conv, conv_other, moments, gain, shift, block, out, block_other, out_other),
        [narrow, narrow, sums],
        [pltpu.VMEM((rows, half), bf16)] * 4 + [pltpu.SemaphoreType.DMA((4,))],
        loaded=4,
    )
    stats = exchange(stats, y_axes)
    count = nzl * nx * nyl
    step = 2 * part // nx
    length = groups * nyh * step
    act, act_other, weight_squares, partial = call(
        functools.partial(weight_kernel, (nx, nyl, nyh)),
        "weight_partial",
        (conv, conv_other, moments, stats, gain, grad, grad_other, activations, acts_other, weight),
        [shape((rows, cin), f32), shape((rows, cin), bf16), shape((8, lanes), f32)],
        [pltpu.VMEM((cin, chunk), f32)]
        + [pltpu.VMEM((cin, rows), bf16)] * 2
        + [pltpu.VMEM((rows, half), bf16)] * 2
        + [pltpu.VMEM((count, length + 16, lanes), bf16)]
        + [pltpu.SemaphoreType.DMA((half // chunk,))],
        written=shape((count, length + 16, lanes), bf16),
    )
    act_grad = (act + swap(act_other).astype(f32)).astype(bf16)
    partial, act_grad = lax.optimization_barrier((exchange(partial, near), act_grad))

    (partial,) = call(
        functools.partial(near_kernel, nyh),
        "near_sum",
        (partial,),
        [shape((nzh * nyh, groups * (step + 2), lanes), bf16)],
        [pltpu.VMEM((length + 16, lanes), f32)],
    )
    (ready,) = call(
        far_kernel,
        "far_sum",
        (exchange(partial, far), weight_squares),
        [shape((2 * nzl * nx, groups * step + 16, lanes), bf16)],
    )
    ready = exchange(ready, ("zl", "x", "c"))
    (squares,) = call(squares_kernel, "squares", (ready,), [shape((ny, 8, lanes), f32)])
    squares = exchange(squares, y_axes)
    new_velocity, gain_grad, shift_grad = call(
        functools.partial(step_kernel, nx),
        "step",
        (ready, squares, conv_weight, velocity),
        [shape((part, cout), f32), shape((1, cout), f32), shape((1, cout), f32)],
    )
    return (act_grad, gain_grad.reshape(cout), shift_grad.reshape(cout), new_velocity)


def solution(mesh, dims=(4, 2, 4, 4, 2, 2)):
    fine = Mesh(mesh.devices.reshape(dims), rep + bn)
    every = P(rep + bn, None)
    return jax.shard_map(
        local,
        mesh=fine,
        in_specs=(every, every, P(bn, None), P(), P(), every, P(bn, None)),
        out_specs=(every, P(), P(), P(bn, None)),
        check_vma=False,
    )
```

```python
import functools

import jax
import jax.numpy as jnp
from jax import lax
from jax.experimental import pallas as pl
from jax.experimental.pallas import tpu as pltpu
from jax.sharding import Mesh, PartitionSpec as P

epsilon = 1e-05
weight_decay = 5e-05
momentum = 0.9
f32, bf16 = jnp.float32, jnp.bfloat16
rep = ("zh", "zl", "x")
y_axes = ("yh", "yl")
bn = ("yh", "yl", "c")
near = ("zl", "x", "yl")
far = ("zh", "yh")
lanes = 128
chunk = 512
groups = chunk // lanes


def swap(value):
    return lax.ppermute(value, "c", [(0, 1), (1, 0)])


def exchange(pieces, axis):
    return lax.all_to_all(pieces, axis, 0, 0, tiled=True)


def copies(value, axis):
    n = lax.axis_size(axis)
    return exchange(jnp.broadcast_to(value[None], (n, *value.shape)), axis)


def fold(row):
    return [row[:, q * lanes : (q + 1) * lanes] for q in range(groups)]


def unfold(tile):
    return jnp.concatenate([tile[q : q + 1] for q in range(groups)], axis=1)


def high_low(value):
    high = value.astype(bf16).astype(f32)
    return high, value - high


def columns(width):
    return [pl.ds(start, chunk) for start in range(0, width, chunk)]


def eighth_kernel(nx, weight, out):
    half = weight.shape[1] // 2
    place = lax.axis_index("zl") * nx + lax.axis_index("x")
    for c in range(2):
        tile = weight[:, pl.ds(pl.multiple_of(c * half + place * lanes, lanes), lanes)]
        for y in range(out.shape[0] // 2):
            out[2 * y + c] = tile


def copies_kernel(block, out, sems):
    writes = [pltpu.make_async_copy(block, out.at[i], sems.at[i]) for i in range(out.shape[0])]
    for write in writes:
        write.start()
    for write in writes:
        write.wait()


def moments_kernel(acts, acts_other, parts, weight, conv, conv_other, moments):
    for i in range(parts.shape[0]):
        weight[:, i * lanes : (i + 1) * lanes] = parts[i]
    count = 2 * conv.shape[0]
    for j, cols in enumerate(columns(conv.shape[1])):
        both = []
        for rows, out in ((acts, conv), (acts_other, conv_other)):
            value = jnp.dot(rows[...], weight[:, cols], preferred_element_type=f32)
            out[:, cols] = value
            both.append(value)
        mean = sum(jnp.sum(value, axis=0, keepdims=True) for value in both) / count
        square = sum(jnp.sum((v - mean) * (v - mean), axis=0, keepdims=True) for v in both)
        tile = jnp.concatenate(fold(mean) + fold(square), axis=0)
        moments[:, 8 * j : 8 * j + 8] = jnp.broadcast_to(tile[None], (moments.shape[0], 8, lanes))


def pooled(moments, rows):
    members = moments.shape[0]
    means, squares = moments[:, :groups], moments[:, groups:]
    mean = jnp.sum(means, axis=0) / members
    offset = means - mean[None]
    square = jnp.sum(squares, axis=0) + rows * jnp.sum(offset * offset, axis=0)
    inv_std = lax.rsqrt(square / (rows * members) + epsilon)
    return unfold(mean), unfold(inv_std)


def stats_kernel(
    conv,
    conv_other,
    moments,
    gain,
    shift,
    block,
    out,
    block_far,
    out_far,
    grad,
    grad_other,
    stats,
    block_other,
    out_other,
    sems,
):
    rows, half = conv.shape
    core = lax.axis_index("c")
    loads = [
        pltpu.make_async_copy(block_far, block_other, sems.at[0]),
        pltpu.make_async_copy(out_far, out_other, sems.at[1]),
    ]
    for load in loads:
        load.start()
    scales = []
    for j, cols in enumerate(columns(half)):
        place = pl.ds(pl.multiple_of(core * half + j * chunk, chunk), chunk)
        mean, inv_std = pooled(moments[:, 8 * j : 8 * j + 8], 2 * rows)
        scales.append((cols, mean, inv_std, gain[:, place] * inv_std, shift[:, place]))

    def sums(of, added, incoming, result, cols, mean, scale, bias):
        centered = of[:, cols] - mean
        summed = centered * scale + bias + added.astype(f32)
        value = jnp.where(summed > 0.0, incoming.astype(f32), 0.0)
        result[:, cols] = value.astype(bf16)
        return (
            jnp.sum(value, axis=0, keepdims=True),
            jnp.sum(value * centered, axis=0, keepdims=True),
        )

    near_sums = [
        sums(conv, block[:, cols], out[:, cols], grad, cols, mean, scale, bias)
        for cols, mean, _, scale, bias in scales
    ]
    for load in loads:
        load.wait()
    for j, (cols, mean, inv_std, scale, bias) in enumerate(scales):
        sum_grad, sum_cross = sums(
            conv_other, block_other[:, cols], out_other[:, cols], grad_other, cols, mean, scale, bias
        )
        sum_grad += near_sums[j][0]
        sum_cross += near_sums[j][1]
        tile = jnp.concatenate(fold(sum_grad) + fold(sum_cross * inv_std), axis=0)
        stats[:, 8 * j : 8 * j + 8] = jnp.broadcast_to(tile[None], (stats.shape[0], 8, lanes))


def weight_kernel(
    sizes,
    conv,
    conv_other,
    moments,
    stats,
    gain,
    grad,
    grad_other,
    acts,
    acts_other,
    weight,
    act,
    act_other,
    squares,
    result_out,
    wide,
    acts_t,
    acts_t_other,
    grad_conv,
    grad_conv_other,
    out,
    sems,
):
    nx, nyl, nyh = sizes
    core = lax.axis_index("c")
    rows, half = conv.shape
    group_rows = 2 * rows * moments.shape[0]
    part = wide.shape[0] // (nyl * nyh)
    step = part // nx
    length = groups * nyh * step
    acts_t[...] = acts[...].T
    acts_t_other[...] = acts_other[...].T
    writes = []
    for j, cols in enumerate(columns(half)):
        place = pl.ds(pl.multiple_of(core * half + j * chunk, chunk), chunk)
        mean, inv_std = pooled(moments[:, 8 * j : 8 * j + 8], 2 * rows)
        sums = jnp.sum(stats[:, 8 * j : 8 * j + 8], axis=0)
        sum_grad, sum_cross = sums[:groups], sums[groups:]
        shift = unfold(sum_grad) / group_rows
        slope = inv_std * unfold(sum_cross) / group_rows
        scale = gain[:, place] * inv_std
        product = 0.0
        for of, pre, left, result in (
            (conv, grad, acts_t, grad_conv),
            (conv_other, grad_other, acts_t_other, grad_conv_other),
        ):
            value = pre[:, cols].astype(f32) - shift - (of[:, cols] - mean) * slope
            narrow = (scale * value).astype(bf16)
            result[:, cols] = narrow
            product += jnp.dot(left[...], narrow, preferred_element_type=f32)
        wide[...] = product
        planes = (*high_low(sum_grad), *high_low(sum_cross))
        for x in range(nx):
            last = jnp.concatenate(
                [planes[x] / (nyl * nyh), jnp.zeros((16 - groups, lanes), f32)], axis=0
            )
            for yl in range(nyl):
                piece = (j * nx + x) * nyl + yl
                rows_of = [
                    wide[
                        pl.ds((yh * nyl + yl) * part + step * x, step), pl.ds(q * lanes, lanes)
                    ]
                    for q in range(groups)
                    for yh in range(nyh)
                ]
                out[piece, :length] = jnp.concatenate(rows_of, axis=0).astype(bf16)
                out[piece, length:] = last.astype(bf16)
        ready = pl.ds(j * nx * nyl, nx * nyl)
        writes.append(pltpu.make_async_copy(out.at[ready], result_out.at[ready], sems.at[j]))
        writes[-1].start()

    dims = (((1,), (1,)), ((), ()))
    act[...] = lax.dot_general(grad_conv[...], weight[...], dims, preferred_element_type=f32)
    act_other[...] = lax.dot_general(
        grad_conv_other[...], weight[...], dims, preferred_element_type=f32
    ).astype(bf16)
    total = jnp.zeros((8, lanes), f32)
    for cols in columns(weight.shape[1]):
        value = weight[:, cols].astype(f32)
        total += sum(fold(jnp.sum((value * value).reshape(-1, 8, chunk), axis=0)))
    squares[...] = total
    for write in writes:
        write.wait()


def near_kernel(nyh, received, out, total):
    total[...] = jnp.sum(received[...].astype(f32), axis=0)
    length = total.shape[0] - 16
    step = length // (groups * nyh)
    tail = high_low(total[length : length + groups, :])
    for yh in range(nyh):
        starts = [(q * nyh + yh) * step for q in range(groups)]
        own = [total[at : at + step, :] for at in starts]
        tile = jnp.concatenate([*own, *tail], axis=0).astype(bf16)
        for zh in range(out.shape[0] // nyh):
            out[zh * nyh + yh] = tile


def spread(value):
    value = jnp.sum(jnp.sum(value, axis=0, keepdims=True), axis=1, keepdims=True)
    return jnp.broadcast_to(value, (1, lanes))


def far_kernel(received, weight_squares, out):
    total = jnp.sum(received[...].astype(f32), axis=0)
    at = total.shape[0] - 2 * groups
    value = total[:at]
    tail = total[at : at + groups] + total[at + groups :]
    square, weight_square = spread(value * value), spread(weight_squares[...])
    last = [*high_low(square), *high_low(weight_square), jnp.zeros((4, lanes), f32)]
    tile = jnp.concatenate([value, *high_low(tail), *last], axis=0).astype(bf16)
    out[...] = jnp.broadcast_to(tile[None], out.shape)


def squares_kernel(parts, squares):
    total = jnp.sum(parts[...].astype(f32), axis=0)
    at = total.shape[0] - 8
    square = total[at : at + 1] + total[at + 1 : at + 2]
    weight_square = (total[at + 2 : at + 3] + total[at + 3 : at + 4]) / (parts.shape[0] // 2)
    tile = jnp.concatenate([square, weight_square, jnp.zeros((6, lanes), f32)], axis=0)
    squares[...] = jnp.broadcast_to(tile[None], squares.shape)


def step_kernel(nx, parts, squares, weight, velocity, out, gain, shift):
    core = lax.axis_index("c")
    half = out.shape[1] // 2
    total = jnp.sum(squares[...], axis=0)
    grad_norm = jnp.sqrt(total[:1, :1])
    weight_norm = jnp.sqrt(total[1:2, :1] / squares.shape[0])
    ratio = weight_norm / (grad_norm + weight_decay * weight_norm)
    count = nx // 2
    for zl in range(parts.shape[0] // (2 * nx)):
        for c in range(2):
            values = [parts[(zl * nx + x) * 2 + c].astype(f32) for x in range(nx)]
            own = [
                parts[(zl * nx + core * count + i) * 2 + c].astype(f32) for i in range(count)
            ]
            step = (own[0].shape[0] - 16) // groups
            for q in range(groups):
                cols = pl.ds(c * half + (zl * groups + q) * lanes, lanes)
                weight_grad = jnp.concatenate([v[q * step : (q + 1) * step] for v in own], axis=0)
                decayed = weight_grad + weight_decay * weight[:, cols].astype(f32)
                out[:, cols] = momentum * velocity[:, cols] + ratio * decayed
                at = groups * step + q
                planes = [v[at : at + 1] + v[at + groups : at + groups + 1] for v in values]
                shift[:, cols] = planes[0] + planes[1]
                gain[:, cols] = planes[2] + planes[3]


def shape(dims, dtype):
    return jax.ShapeDtypeStruct(dims, dtype)


def whole(dims):
    return pl.BlockSpec(dims, lambda j: (0,) * len(dims))


def params(mib=24):
    return pltpu.CompilerParams(vmem_limit_bytes=mib << 20)


def call(kernel, name, operands, outs, scratch=(), loaded=0, written=None):
    anywhere = pl.BlockSpec(memory_space=pl.ANY)
    at = len(operands) - loaded
    in_specs = [whole(value.shape) for value in operands[:at]] + [anywhere] * loaded
    out_specs = [whole(out.shape) for out in outs]
    if written is not None:
        out_specs.append(anywhere)
        outs = [*outs, pltpu.HBM(written.shape, written.dtype)]
    return pl.pallas_call(
        kernel,
        grid=(1,),
        in_specs=in_specs,
        out_specs=out_specs,
        out_shape=outs,
        scratch_shapes=scratch,
        compiler_params=params(),
        name=name,
    )(*operands)


def local(block_input, activations, conv_weight, bn_gain, bn_shift, out_grad, velocity):
    rows, cin = activations.shape
    part, cout = conv_weight.shape
    half = cout // 2
    nzh, nzl, nx = (lax.axis_size(a) for a in rep)
    nyh, nyl = (lax.axis_size(a) for a in y_axes)
    ny = nyh * nyl
    members = 2 * ny
    first_core = lax.axis_index("c") == 0
    gain, shift = bn_gain.reshape(1, cout), bn_shift.reshape(1, cout)

    def halves(value):
        low, high = value[:, :half], value[:, half:]
        return jnp.where(first_core, low, high), jnp.where(first_core, high, low)

    (eighth,) = call(
        functools.partial(eighth_kernel, nx),
        "eighth",
        (conv_weight,),
        [shape((members, part, lanes), bf16)],
    )
    eighth = exchange(eighth, bn).reshape(cin, lanes)
    (spread_out,) = call(
        copies_kernel,
        "weight_copies",
        (eighth,),
        [],
        [pltpu.SemaphoreType.DMA((nzl * nx,))],
        written=shape((nzl * nx, cin, lanes), bf16),
    )
    weight_parts = exchange(spread_out, ("zl", "x"))
    acts_other = swap(activations)
    block, block_other = halves(block_input)
    out, out_other = halves(out_grad)
    block_other, out_other = swap(block_other), swap(out_other)
    weight_parts, acts_other, block, out = lax.optimization_barrier(
        (weight_parts, acts_other, block, out)
    )

    wide = shape((rows, half), f32)
    narrow = shape((rows, half), bf16)
    sums = shape((ny, 2 * half // lanes, lanes), f32)
    weight, conv, conv_other, moments = call(
        moments_kernel,
        "moments",
        (activations, acts_other, weight_parts),
        [shape((cin, half), bf16), wide, wide, sums],
    )
    moments, block_other, out_other = lax.optimization_barrier((moments, block_other, out_other))
    moments = exchange(moments, y_axes)
    grad, grad_other, stats = call(
        stats_kernel,
        "stats",
        (conv, conv_other, moments, gain, shift, block, out, block_other, out_other),
        [narrow, narrow, sums],
        [pltpu.VMEM((rows, half), bf16)] * 2 + [pltpu.SemaphoreType.DMA((2,))],
        loaded=2,
    )
    stats = exchange(stats, y_axes)
    count = nzl * nx * nyl
    step = 2 * part // nx
    length = groups * nyh * step
    act, act_other, weight_squares, partial = call(
        functools.partial(weight_kernel, (nx, nyl, nyh)),
        "weight_partial",
        (conv, conv_other, moments, stats, gain, grad, grad_other, activations, acts_other, weight),
        [shape((rows, cin), f32), shape((rows, cin), bf16), shape((8, lanes), f32)],
        [pltpu.VMEM((cin, chunk), f32)]
        + [pltpu.VMEM((cin, rows), bf16)] * 2
        + [pltpu.VMEM((rows, half), bf16)] * 2
        + [pltpu.VMEM((count, length + 16, lanes), bf16)]
        + [pltpu.SemaphoreType.DMA((half // chunk,))],
        written=shape((count, length + 16, lanes), bf16),
    )
    act_grad = (act + swap(act_other).astype(f32)).astype(bf16)
    partial, act_grad = lax.optimization_barrier((exchange(partial, near), act_grad))

    (partial,) = call(
        functools.partial(near_kernel, nyh),
        "near_sum",
        (partial,),
        [shape((nzh * nyh, groups * (step + 2), lanes), bf16)],
        [pltpu.VMEM((length + 16, lanes), f32)],
    )
    (ready,) = call(
        far_kernel,
        "far_sum",
        (exchange(partial, far), weight_squares),
        [shape((2 * nzl * nx, groups * step + 16, lanes), bf16)],
    )
    ready = exchange(ready, ("zl", "x", "c"))
    (squares,) = call(squares_kernel, "squares", (ready,), [shape((ny, 8, lanes), f32)])
    squares = exchange(squares, y_axes)
    new_velocity, gain_grad, shift_grad = call(
        functools.partial(step_kernel, nx),
        "step",
        (ready, squares, conv_weight, velocity),
        [shape((part, cout), f32), shape((1, cout), f32), shape((1, cout), f32)],
    )
    return (act_grad, gain_grad.reshape(cout), shift_grad.reshape(cout), new_velocity)


def solution(mesh, dims=(4, 2, 4, 4, 2, 2)):
    fine = Mesh(mesh.devices.reshape(dims), rep + bn)
    every = P(rep + bn, None)
    return jax.shard_map(
        local,
        mesh=fine,
        in_specs=(every, every, P(bn, None), P(), P(), every, P(bn, None)),
        out_specs=(every, P(), P(), P(bn, None)),
        check_vma=False,
    )
```
